32 devices in a mesh: seq: 16 (over z, y, x), head: 2 (over core).
Axes of the slice: x: 2, y: 2, z: 4, core: 2. Of those that a mesh axis runs over, the one named last changes fastest.
Arguments:
- x_in: bfloat16 [4096, 2048], P('seq', 'head'), may hold values from -45 to 45
- gate_in: bfloat16 [4096, 2048], P('seq', 'head'), may hold values from -6 to 6
- b_in: bfloat16 [4096, 128], P('seq'), may hold values from -0.375 to 0.375
- c_in: bfloat16 [4096, 128], P('seq'), may hold values from -0.375 to 0.375
- decay_fwd: float32 [32, 4096], P('head', 'seq'), may hold values from -1 to 0
- decay_bwd: float32 [32, 4096], P('head', 'seq'), may hold values from -1 to 0
- skip_gain: float32 [32], P('head'), may hold values from 0.5 to 1.5
- norm_gain: float32 [2048], P('head'), may hold values from 0.1 to 1.9
- w_out: bfloat16 [2048, 1024], P('head'), may hold values from -0.125 to 0.125
- d_out: bfloat16 [4096, 1024], P('seq'), may hold values from -6 to 6
Outputs:
- grad_x: bfloat16 [4096, 2048], P('seq', 'head')
- grad_z: bfloat16 [4096, 2048], P('seq', 'head')
- grad_b: float32 [4096, 128], P('seq')
- grad_c: float32 [4096, 128], P('seq')
- grad_w: float32 [2048, 1024], P('head')
The draws below stay inside these ranges and needn't reach their ends.
All inputs are finite; a program needn't handle non-finite values.
Results may differ from the reference program's by a relative error of at most 0.0029.
Values sent between devices are 32-bit elements; how exact they have to be, the bound alone decides.
A program may use at most 64 MiB of HBM per device.

```python
import math
import jax
import jax.numpy as jnp
from jax import lax

DM = 1024
STATE_HEADS = 32
HEAD_DIM = 64
STATE = 128
FR_DEV = 256
INNER = 2048
WINDOW_FRAMES = 4096


def draw_x_in(key, part):
    random_keys = jax.random.split(key, 3)
    column = 0.3 * jnp.exp(jax.random.uniform(random_keys[0], (INNER,), jnp.float32, 0.0, math.log(10.0)))
    head_place = (jnp.arange(INNER) // HEAD_DIM).astype(jnp.float32) / max(STATE_HEADS - 1, 1)
    rising = jnp.exp(0.5 * math.log(3.0) * head_place)
    row_scale = jnp.exp(jax.random.uniform(random_keys[1], (WINDOW_FRAMES, 1), jnp.float32, -math.log(2.0), math.log(2.0)))
    base = jnp.clip(jax.random.normal(random_keys[2], (WINDOW_FRAMES, INNER), jnp.float32), -4.0, 4.0)
    return (base * column[None, :] * rising[None, :] * row_scale).astype(jnp.bfloat16)


def log_decays(key):
    random_keys = jax.random.split(key, 7)
    fast_cut = 4
    fast_heads = jax.random.randint(random_keys[0], (STATE_HEADS, 1), 0, 8) < fast_cut
    fast_rate = jnp.exp(jax.random.uniform(random_keys[1], (STATE_HEADS, 1), jnp.float32, math.log(1.0 / 50.0), math.log(1.0 / 30.0)))
    slow_rate = jnp.exp(jax.random.uniform(random_keys[2], (STATE_HEADS, 1), jnp.float32, math.log(0.2), math.log(1.0))) / WINDOW_FRAMES
    decay_rate = jnp.where(fast_heads, fast_rate, slow_rate)
    random_offset = jnp.exp(jax.random.uniform(random_keys[3], (STATE_HEADS, WINDOW_FRAMES), jnp.float32, -math.log(2.0), math.log(2.0)))
    tile_multiplier = jnp.exp(jax.random.uniform(random_keys[4], (STATE_HEADS, WINDOW_FRAMES // FR_DEV, 1), jnp.float32, -math.log(2.0), math.log(2.0)))
    tile_multiplier = jnp.broadcast_to(tile_multiplier, (STATE_HEADS, WINDOW_FRAMES // FR_DEV, FR_DEV)).reshape(STATE_HEADS, WINDOW_FRAMES)
    spike_mask = jax.random.randint(random_keys[5], (STATE_HEADS, WINDOW_FRAMES), 0, WINDOW_FRAMES) < 2
    spike_length = jnp.log(jax.random.uniform(random_keys[6], (STATE_HEADS, WINDOW_FRAMES), jnp.float32, 0.6, 0.8))
    return -(decay_rate * random_offset * tile_multiplier) + jnp.where(spike_mask, spike_length, 0.0)


def draw_decay_fwd(key, part):
    return log_decays(jax.random.fold_in(key, 11))


def draw_decay_bwd(key, part):
    return log_decays(jax.random.fold_in(key, 12))


def shard_levels(stream_key, shape, cuts, smallest, top_value):
    gain, own = 1.0, jax.random.fold_in(stream_key, 6)
    for axis_at, parts in cuts:
        steps = jnp.exp(jax.random.uniform(jax.random.fold_in(own, axis_at), (parts,), jnp.float32, smallest / len(cuts), top_value / len(cuts)))
        gain = gain * jnp.repeat(steps, shape[axis_at] // parts).reshape([-1 if axis == axis_at else 1 for axis in range(len(shape))])
    return gain


def scatter_about(rng, dims, scale, bound, cuts=(), held_as=jnp.bfloat16):
    drawn = jax.random.normal(rng, dims, jnp.float32) * scale
    if len(cuts) > 0:
        drawn = shard_levels(rng, dims, cuts, -0.22, 0.18) * drawn
    return jnp.clip(drawn, min=-bound, max=bound).astype(held_as)


def setup_inputs(seed: int = 0) -> dict:
    splits = jax.random.split(jax.random.key(seed), 11)
    return {
        "x_in": draw_x_in(jax.random.fold_in(splits[10], 71), 0),
        "gate_in": scatter_about(splits[1], (WINDOW_FRAMES, INNER), 1.0, 6.0, ((0, 16), (1, 2))),
        "b_in": scatter_about(splits[2], (WINDOW_FRAMES, STATE), 256 ** -0.5, 0.375, ((0, 16),)),
        "c_in": scatter_about(splits[3], (WINDOW_FRAMES, STATE), 256 ** -0.5, 0.375, ((0, 16),)),
        "decay_fwd": draw_decay_fwd(jax.random.fold_in(splits[10], 71), 0),
        "decay_bwd": draw_decay_bwd(jax.random.fold_in(splits[10], 71), 0),
        "skip_gain": jnp.clip(0.5 + 1.0 * jax.random.uniform(splits[6], (STATE_HEADS,), jnp.float32) ** shard_levels(splits[6], (STATE_HEADS,), ((0, 2),), -0.2, 0.2), 0.5, 1.5),
        "norm_gain": jnp.clip(1.0 + 0.18 * jax.random.normal(splits[7], (INNER,), jnp.float32), 0.1, 1.9),
        "w_out": scatter_about(splits[8], (INNER, DM), INNER ** -0.5, 0.125, ((0, 2),)),
        "d_out": scatter_about(splits[9], (WINDOW_FRAMES, DM), 1.0, 6.0, ((0, 16),)),
    }


exact_mode = lax.Precision.HIGHEST
eps_norm = 1e-05
weight_scale = 0.0078125

def group_step(carry_state, pieces):
    signal, b_rows, c_rows, log_rates = pieces
    cumul = jnp.cumsum(log_rates, axis=1)
    spread = cumul[:, :, None] - cumul[:, None, :]
    positions = jnp.arange(log_rates.shape[1])
    causal_mask = positions[:, None] >= positions[None, :]
    weights = jnp.exp(jnp.where(causal_mask[None], spread, -jnp.inf))
    scores = jnp.dot(c_rows, b_rows.T, precision=exact_mode)
    within = jnp.einsum('hts,shp->thp', weights * scores[None], signal, precision=exact_mode)
    across = jnp.einsum('tn,hpn->thp', c_rows, carry_state, precision=exact_mode) * jnp.exp(cumul).T[:, :, None]
    end_total = cumul[:, -1]
    tail_rate = jnp.exp(end_total[:, None] - cumul)
    fresh_state = jnp.einsum('hs,shp,sn->hpn', tail_rate, signal, b_rows, precision=exact_mode)
    next_state = jnp.exp(end_total)[:, None, None] * carry_state + fresh_state
    return (next_state, within + across)

def causal(signal, b_rows, c_rows, log_rates):
    blocks = signal.shape[0] // FR_DEV
    signal_blocks = signal.reshape(blocks, FR_DEV, STATE_HEADS, HEAD_DIM)
    b_blocks = b_rows.reshape(blocks, FR_DEV, STATE)
    c_blocks = c_rows.reshape(blocks, FR_DEV, STATE)
    rate_blocks = log_rates.reshape(STATE_HEADS, blocks, FR_DEV).transpose(1, 0, 2)
    initial = jnp.zeros((STATE_HEADS, HEAD_DIM, STATE), jnp.float32)
    _, outputs = lax.scan(jax.checkpoint(group_step), initial, (signal_blocks, b_blocks, c_blocks, rate_blocks))
    return outputs.reshape(signal.shape)

def anticausal(signal, b_rows, c_rows, log_rates):
    flipped = causal(jnp.flip(signal, 0), jnp.flip(b_rows, 0), jnp.flip(c_rows, 0), jnp.flip(log_rates, 1))
    return jnp.flip(flipped, 0)

def reference(x_in, gate_in, b_in, c_in, decay_fwd, decay_bwd, skip_gain, norm_gain, w_out, d_out):
    signal = x_in.astype(jnp.float32).reshape(WINDOW_FRAMES, STATE_HEADS, HEAD_DIM)
    b_rows = b_in.astype(jnp.float32)
    c_rows = c_in.astype(jnp.float32)

    def branches(sig_vals, b_vals, c_vals):
        return causal(sig_vals, b_vals, c_vals, decay_fwd) + anticausal(sig_vals, b_vals, c_vals, decay_bwd)
    ssd_out, pullback = jax.vjp(branches, signal, b_rows, c_rows)
    merged = (ssd_out + skip_gain[None, :, None] * signal).reshape(WINDOW_FRAMES, INNER)
    gate_rows = gate_in.astype(jnp.float32)
    sigmoid_z = jax.nn.sigmoid(gate_rows)
    gated_y = merged * gate_rows * sigmoid_z
    inv_rms = lax.rsqrt(lax.optimization_barrier(jnp.mean(gated_y * gated_y, axis=1, keepdims=True)) + eps_norm)
    normed = gated_y * inv_rms * norm_gain
    grad_w = jnp.dot(normed.astype(jnp.bfloat16).T, d_out, preferred_element_type=jnp.float32) * weight_scale
    grad_n = jnp.dot(d_out, w_out.T, preferred_element_type=jnp.float32)
    scaled = grad_n * norm_gain
    cross_mean = lax.optimization_barrier(jnp.mean(gated_y * scaled, axis=1, keepdims=True))
    grad_g = inv_rms * scaled - gated_y * inv_rms * inv_rms * inv_rms * cross_mean
    grad_y = grad_g * gate_rows * sigmoid_z
    grad_z = grad_g * merged * sigmoid_z * (1.0 + gate_rows * (1.0 - sigmoid_z))
    grad_rows = grad_y.reshape(WINDOW_FRAMES, STATE_HEADS, HEAD_DIM)
    grad_sig, grad_b, grad_c = pullback(grad_rows)
    grad_x = (grad_sig + skip_gain[None, :, None] * grad_rows).reshape(WINDOW_FRAMES, INNER)
    return (grad_x.astype(jnp.bfloat16), grad_z.astype(jnp.bfloat16), grad_b, grad_c, grad_w)
```

```python
import functools

import jax
import jax.numpy as jnp
from jax import lax
from jax.experimental import pallas as pl
from jax.experimental.pallas import tpu as pltpu
from jax.sharding import PartitionSpec as P

HEAD_DIM = 64
PAIR = 2 * HEAD_DIM
QUAD = 4
F32 = jnp.float32
BF16 = jnp.bfloat16
eps_norm = 1e-05
weight_scale = 0.0078125
VMEM_BYTES = 48 * 1024 * 1024


def dot(a, b, ca, cb):
    return lax.dot_general(a, b, (((ca,), (cb,)), ((), ())), preferred_element_type=F32)


def split(a):
    high = a.astype(BF16)
    return high, (a - high.astype(F32)).astype(BF16)


def dot_split_left(a, b, ca, cb):
    high, low = split(a)
    return dot(high, b, ca, cb) + dot(low, b, ca, cb)


def dot_split_right(a, b, ca, cb):
    high, low = split(b)
    return dot(a, high, ca, cb) + dot(a, low, ca, cb)


def dot_split_both(a, b, ca, cb):
    a_high, a_low = split(a)
    b_high, b_low = split(b)
    return dot(a_high, b_high, ca, cb) + (dot(a_high, b_low, ca, cb) + dot(a_low, b_high, ca, cb))


def by_head(first, second, frames):
    lane = lax.broadcasted_iota(jnp.int32, (frames, PAIR), 1)
    return jnp.where(lane < HEAD_DIM, first, second)


def pair_column(cols, at, frames):
    return by_head(cols[:, at : at + 1], cols[:, 4 + at : 5 + at], frames)


def pair_weights(cols, rows, e, frames, later_rows):
    f_col, b_col = cols[:, 4 * e : 4 * e + 1], cols[:, 4 * e + 1 : 4 * e + 2]
    f_row, b_row = rows[4 * e : 4 * e + 1, :], rows[4 * e + 1 : 4 * e + 2, :]
    i = lax.broadcasted_iota(jnp.int32, (frames, frames), 0)
    j = lax.broadcasted_iota(jnp.int32, (frames, frames), 1)
    if later_rows:
        power = jnp.where(i >= j, f_col - f_row, b_row - b_col)
    else:
        power = jnp.where(j >= i, f_row - f_col, b_col - b_row)
    weight = jnp.exp(power)
    return jnp.where(i == j, 2.0 * weight, weight)


def state_kernel(x_ref, b_ref, cols_ref, out_ref):
    frames = x_ref.shape[0]
    cols = cols_ref[0]
    x = x_ref[...].astype(F32)
    tail = jnp.exp(pair_column(cols, 2, frames))
    lead = jnp.exp(pair_column(cols, 1, frames))
    out_ref[0] = dot_split_left(x * tail, b_ref[...], 0, 0)
    out_ref[1] = dot_split_left(x * lead, b_ref[...], 0, 0)


def within_kernel(x_ref, b_ref, c_ref, cols_ref, rows_ref, w_ref, d_ref, gain_ref, skip_ref,
                  y_ref, m_ref, scores):
    frames = x_ref.shape[0]

    @pl.when(pl.program_id(0) == 0)
    def _():
        scores[...] = dot(c_ref[...], b_ref[...], 1, 1)

    cols, rows = cols_ref[0], rows_ref[0]
    x = x_ref[...]
    parts = []
    for e in range(2):
        pw = pair_weights(cols, rows, e, frames, True) * scores[...]
        parts.append(dot_split_left(pw, x, 1, 0))
    y_ref[...] = by_head(parts[0], parts[1], frames) + skip_ref[...] * x.astype(F32)
    m_ref[...] = dot(d_ref[...], w_ref[...], 1, 1) * gain_ref[...]


def merge_kernel(near_ref, m_ref, z_ref, c_ref, cols_ref, entry_ref, y_ref, sums_ref, sq, cross):
    frames = near_ref.shape[0]
    step = pl.program_id(0)

    @pl.when(step == 0)
    def _():
        sq[...] = jnp.zeros_like(sq)
        cross[...] = jnp.zeros_like(cross)

    cols = cols_ref[0]
    c = c_ref[...]
    y = near_ref[...]
    y = y + jnp.exp(pair_column(cols, 0, frames)) * dot_split_right(c, entry_ref[0], 1, 1)
    y = y + jnp.exp(pair_column(cols, 3, frames)) * dot_split_right(c, entry_ref[1], 1, 1)
    y_ref[...] = y
    z = z_ref[...].astype(F32)
    u = y * z * (1.0 / (1.0 + jnp.exp(-z)))
    sq[...] += u * u
    cross[...] += u * m_ref[...]

    @pl.when(step == pl.num_programs(0) - 1)
    def _():
        sums_ref[:, 0:1] = jnp.sum(sq[...], axis=1, keepdims=True)
        sums_ref[:, 1:2] = jnp.sum(cross[...], axis=1, keepdims=True)


def turn_kernel(inner, y_ref, m_ref, z_ref, c_ref, cols_ref, sums_ref, gain_ref, d_ref,
                dy_ref, gz_ref, back_ref, *w_refs):
    frames = y_ref.shape[0]
    cols = cols_ref[0]
    y = y_ref[...]
    z = z_ref[...].astype(F32)
    sig = 1.0 / (1.0 + jnp.exp(-z))
    silu = z * sig
    u = y * silu
    q = lax.rsqrt(sums_ref[:, 0:1] * (1.0 / inner) + eps_norm)
    k = sums_ref[:, 1:2] * (1.0 / inner)
    du = q * m_ref[...] - u * (q * q * q * k)
    dy = du * silu
    dy_ref[...] = dy
    gz_ref[...] = (du * y * sig * (1.0 + z * (1.0 - sig))).astype(BF16)
    n = (u * q * gain_ref[...]).astype(BF16)
    c = c_ref[...]
    back_ref[0] = dot_split_left(dy * jnp.exp(pair_column(cols, 0, frames)), c, 0, 0)
    back_ref[1] = dot_split_left(dy * jnp.exp(pair_column(cols, 3, frames)), c, 0, 0)
    at = 0
    for w_ref in w_refs:
        columns = w_ref.shape[1]
        w_ref[...] = dot(n, d_ref[:, at : at + columns], 0, 0) * weight_scale
        at += columns


def near_kernel(x_ref, b_ref, c_ref, cols_ref, rows_ref, skip_ref, dy_ref, entry_ref,
                gx_ref, gb_ref, gc_ref, scores, pairs):
    frames = x_ref.shape[0]
    step = pl.program_id(0)

    @pl.when(step == 0)
    def _():
        scores[...] = dot(b_ref[...], c_ref[...], 1, 1)
        pairs[...] = jnp.zeros_like(pairs)
        gc_ref[...] = jnp.zeros_like(gc_ref)

    cols, rows = cols_ref[0], rows_ref[0]
    x = x_ref[...]
    dy = dy_ref[...]
    lane = lax.broadcasted_iota(jnp.int32, (frames, PAIR), 1)
    parts = []
    for e in range(2):
        weight = pair_weights(cols, rows, e, frames, False)
        own = (lane < HEAD_DIM) if e == 0 else (lane >= HEAD_DIM)
        dy_own = jnp.where(own, dy, 0.0)
        pairs[...] += weight * dot_split_right(x, dy_own, 1, 1)
        parts.append(dot_split_both(weight * scores[...], dy_own, 1, 0))
    gx_ref[...] = parts[0] + parts[1] + skip_ref[...] * dy
    gc_ref[...] += dot_split_both(dy * jnp.exp(pair_column(cols, 0, frames)), entry_ref[0], 1, 0)
    gc_ref[...] += dot_split_both(dy * jnp.exp(pair_column(cols, 3, frames)), entry_ref[1], 1, 0)

    @pl.when(step == pl.num_programs(0) - 1)
    def _():
        gb_ref[...] = dot_split_left(pairs[...], c_ref[...], 1, 0)
        gc_ref[...] += dot_split_left(pairs[...], b_ref[...], 0, 0)


def far_kernel(x_ref, b_ref, cols_ref, exit_ref, near_ref, gb_near_ref, gx_ref, gb_ref):
    frames = x_ref.shape[0]

    @pl.when(pl.program_id(0) == 0)
    def _():
        gb_ref[...] = gb_near_ref[...]

    cols = cols_ref[0]
    b = b_ref[...]
    x = x_ref[...].astype(F32)
    tail = jnp.exp(pair_column(cols, 2, frames))
    lead = jnp.exp(pair_column(cols, 1, frames))
    far = tail * dot_split_right(b, exit_ref[0], 1, 1) + lead * dot_split_right(b, exit_ref[1], 1, 1)
    gx_ref[...] = (near_ref[...] + far).astype(BF16)
    gb_ref[...] += dot_split_both(x * tail, exit_ref[0], 1, 0)
    gb_ref[...] += dot_split_both(x * lead, exit_ref[1], 1, 0)


def call(kernel, name, grid, ins, in_specs, outs, out_specs, scratch=(), flops=0):
    moved = sum(a.size * a.dtype.itemsize for a in ins) + sum(
        o.size * o.dtype.itemsize for o in outs)
    return pl.pallas_call(
        kernel,
        name=name,
        grid=(grid,),
        in_specs=in_specs,
        out_specs=out_specs,
        out_shape=outs,
        scratch_shapes=list(scratch),
        compiler_params=pltpu.CompilerParams(
            dimension_semantics=("arbitrary",), vmem_limit_bytes=VMEM_BYTES),
        cost_estimate=pl.CostEstimate(flops=flops, bytes_accessed=moved, transcendentals=0),
    )(*ins)


def sum_over(value, axis):
    size = lax.axis_size(axis)
    reach = 1
    while reach < size:
        value = value + lax.ppermute(value, axis, [(i, i ^ reach) for i in range(size)])
        reach *= 2
    return value


def sum_slabs(value, bits):
    size, me = lax.axis_size("seq"), lax.axis_index("seq")
    for bit in bits:
        mine = (me >> bit) & 1
        halves = value.reshape(2, value.shape[0] // 2, value.shape[1])
        sent = lax.dynamic_index_in_dim(halves, 1 - mine, 0, keepdims=False)
        came = lax.ppermute(sent, "seq", [(i, i ^ (1 << bit)) for i in range(size)])
        value = lax.dynamic_index_in_dim(halves, mine, 0, keepdims=False) + came
    for bit in reversed(bits):
        mine = (me >> bit) & 1
        came = lax.ppermute(value, "seq", [(i, i ^ (1 << bit)) for i in range(size)])
        first = jnp.where(mine == 0, value, came)
        second = jnp.where(mine == 0, came, value)
        value = jnp.concatenate([first, second], axis=0)
    return value


def carry(up, up_logs, down, down_logs):
    size, me = lax.axis_size("seq"), lax.axis_index("seq")
    groups = size // QUAD
    q, g = me % QUAD, me // QUAD
    rows, width = up.shape
    heads = up_logs.shape[1]
    part, part_heads = rows // QUAD, heads // QUAD
    both = jnp.stack([up, down]).reshape(2, QUAD, part, width)

    def block(r):
        return lax.dynamic_index_in_dim(both, q ^ r, 1, keepdims=False)

    held = [block(0)] + [
        lax.ppermute(block(r), "seq", [(i, i ^ r) for i in range(size)]) for r in range(1, QUAD)]

    def my_logs(logs):
        mine = lax.dynamic_slice_in_dim(logs, q * part_heads, part_heads, 1)
        return mine.reshape(groups, QUAD, part_heads)

    def scale(logs, state):
        factor = jnp.exp(logs)[:, None, None]
        return (factor * state.reshape(part_heads, -1, width)).reshape(part, width)

    answers = []
    for k, logs in ((0, my_logs(up_logs)), (1, my_logs(down_logs))):
        rising = k == 0

        def ahead(a, b):
            return (a > b) if rising else (a < b)

        own = lax.dynamic_index_in_dim(logs, g, 0, keepdims=False)
        place = jnp.arange(QUAD)
        group_logs = jnp.sum(logs, axis=1)

        def between(low, high):
            keep = jnp.ones((QUAD,), bool)
            if low is not None:
                keep = keep & ahead(place, low)
            if high is not None:
                keep = keep & ahead(high, place)
            return jnp.sum(jnp.where(keep[:, None], own, 0.0), axis=0)

        states = [held[r][k] for r in range(QUAD)]
        total = sum(scale(between(q ^ r, None), states[r]) for r in range(QUAD))
        group_place = jnp.arange(groups)
        sign = 1 if rising else -1
        whole = lax.dynamic_index_in_dim(group_logs, g, 0, keepdims=False)
        entering = None
        reach = 1
        while reach < groups:
            sent = total if entering is None else total + scale(whole, entering)
            moves = [(i, i + sign * reach * QUAD) for i in range(size)
                     if 0 <= i + sign * reach * QUAD < size]
            came = lax.ppermute(sent, "seq", moves)
            if entering is None:
                entering = came
            else:
                steps = (g - group_place) * sign
                keep = (steps >= 1) & (steps < reach)
                passed = jnp.sum(jnp.where(keep[:, None], group_logs, 0.0), axis=0)
                entering = entering + scale(passed, came)
            reach *= 2
        replies = []
        for r in range(QUAD):
            reply = scale(between(None, q ^ r), entering)
            for s in range(QUAD):
                if s != r:
                    term = scale(between(q ^ s, q ^ r), states[s])
                    reply = reply + jnp.where(ahead(q ^ r, q ^ s), term, 0.0)
            replies.append(reply)
        answers.append(replies)
    full = jnp.zeros((2, QUAD, part, width), F32)
    for r in range(QUAD):
        reply = jnp.stack([answers[0][r], answers[1][r]])
        if r:
            reply = lax.ppermute(reply, "seq", [(i, i ^ r) for i in range(size)])
        full = lax.dynamic_update_slice_in_dim(full, reply[:, None], q ^ r, 1)
    return full.reshape(2, rows, width)


def body(x_in, gate_in, b_in, c_in, decay_fwd, decay_bwd, skip_gain, norm_gain, w_out, d_out):
    frames, width = x_in.shape
    heads = decay_fwd.shape[0]
    state = b_in.shape[1]
    model = d_out.shape[1]
    pairs = heads // 2
    inner = width * lax.axis_size("head")

    fwd = jnp.cumsum(decay_fwd, axis=1)
    bwd = jnp.cumsum(decay_bwd, axis=1) - decay_bwd
    fwd_end = fwd[:, -1:]
    bwd_end = bwd[:, -1:] + decay_bwd[:, -1:]
    lines = jnp.stack([fwd, bwd, fwd_end - fwd, bwd_end - bwd], axis=1)
    rows = lines.reshape(pairs, 8, frames)
    cols = rows.transpose(0, 2, 1)
    ends = lax.all_gather(jnp.stack([fwd_end[:, 0], bwd_end[:, 0]]), "seq")
    logs_f, logs_b = ends[:, 0], ends[:, 1]
    skip = jnp.repeat(skip_gain, HEAD_DIM)[None, :]
    gain = norm_gain[None, :]

    wide = pl.BlockSpec((frames, PAIR), lambda i: (0, i))
    narrow = pl.BlockSpec((frames, state), lambda i: (0, 0))
    col = pl.BlockSpec((1, frames, 8), lambda i: (i, 0, 0))
    row = pl.BlockSpec((1, 8, frames), lambda i: (i, 0, 0))
    lanes = pl.BlockSpec((1, PAIR), lambda i: (0, i))
    states = pl.BlockSpec((2, PAIR, state), lambda i: (0, i, 0))
    model_rows = pl.BlockSpec((frames, model), lambda i: (0, 0))
    weight_rows = pl.BlockSpec((PAIR, model), lambda i: (i, 0))
    sums_spec = pl.BlockSpec((frames, 2), lambda i: (0, 0))
    shape = jax.ShapeDtypeStruct
    wide_f32, wide_bf16 = shape((frames, width), F32), shape((frames, width), BF16)
    state_out, narrow_out = shape((2, width, state), F32), shape((frames, state), F32)
    square = pltpu.VMEM((frames, frames), F32)
    lane_sums = pltpu.VMEM((frames, PAIR), F32)
    quad_flops = 2 * frames * frames * width

    local = call(state_kernel, "local_states", pairs, (x_in, b_in, cols), [wide, narrow, col],
                 [state_out], [states], flops=8 * frames * width * state)[0]
    entry = carry(local[0], logs_f, local[1], logs_b)
    near_y, scaled = call(
        within_kernel, "within_slab", pairs,
        (x_in, b_in, c_in, cols, rows, w_out, d_out, gain, skip),
        [wide, narrow, narrow, col, row, weight_rows, model_rows, lanes, lanes],
        [wide_f32, wide_f32], [wide, wide], [square],
        flops=8 * quad_flops + 2 * frames * width * model)
    y, sums = call(
        merge_kernel, "merge_entry", pairs, (near_y, scaled, gate_in, c_in, cols, entry),
        [wide, wide, wide, narrow, col, states],
        [wide_f32, shape((frames, 2), F32)], [wide, sums_spec], [lane_sums, lane_sums],
        flops=8 * frames * width * state)
    sums = sum_over(sums, "head")
    bits = list(range((lax.axis_size("seq") - 1).bit_length()))
    orders = (bits, [bits[1], bits[0]] + bits[2:], bits[2:] + bits[:2])
    thirds = model // 8 * 3
    chunks = (thirds, thirds, model - 2 * thirds)
    dy, grad_z, back, *local_w = call(
        functools.partial(turn_kernel, inner), "norm_backward", pairs,
        (y, scaled, gate_in, c_in, cols, sums, gain, d_out),
        [wide, wide, wide, narrow, col, sums_spec, lanes, model_rows],
        [wide_f32, wide_bf16, state_out] + [shape((width, n), F32) for n in chunks],
        [wide, wide, states] + [pl.BlockSpec((PAIR, n), lambda i: (i, 0)) for n in chunks],
        flops=2 * frames * width * model + 8 * frames * width * state)
    exits = carry(back[1], logs_b, back[0], logs_f)
    grad_w = jnp.concatenate(
        [sum_slabs(part, order) for part, order in zip(local_w, orders)], axis=1)
    near_x, near_b, grad_c = call(
        near_kernel, "near_gradients", pairs,
        (x_in, b_in, c_in, cols, rows, skip, dy, entry),
        [wide, narrow, narrow, col, row, lanes, wide, states],
        [wide_f32, narrow_out, narrow_out], [wide, narrow, narrow], [square, square],
        flops=20 * quad_flops)
    grad_c = sum_over(grad_c, "head")
    exits = jnp.stack([exits[1], exits[0]])
    grad_x, grad_b = call(
        far_kernel, "far_gradients", pairs, (x_in, b_in, cols, exits, near_x, near_b),
        [wide, narrow, col, states, wide, narrow],
        [wide_bf16, narrow_out], [wide, narrow], flops=20 * frames * width * state)
    grad_b = sum_over(grad_b, "head")
    return grad_x, grad_z, grad_b, grad_c, grad_w


def solution(mesh):
    in_specs = (
        P("seq", "head"),
        P("seq", "head"),
        P("seq", None),
        P("seq", None),
        P("head", "seq"),
        P("head", "seq"),
        P("head"),
        P("head"),
        P("head", None),
        P("seq", None),
    )
    out_specs = (
        P("seq", "head"),
        P("seq", "head"),
        P("seq", None),
        P("seq", None),
        P("head", None),
    )
    return jax.shard_map(body, mesh=mesh, in_specs=in_specs, out_specs=out_specs, check_vma=False)
```

```python
import functools

import jax
import jax.numpy as jnp
from jax import lax
from jax.experimental import pallas as pl
from jax.experimental.pallas import tpu as pltpu
from jax.sharding import PartitionSpec as P

HEAD_DIM = 64
PAIR = 2 * HEAD_DIM
QUAD = 4
F32 = jnp.float32
BF16 = jnp.bfloat16
eps_norm = 1e-05
weight_scale = 0.0078125
VMEM_BYTES = 48 * 1024 * 1024


def dot(a, b, ca, cb):
    return lax.dot_general(a, b, (((ca,), (cb,)), ((), ())), preferred_element_type=F32)


def split(a):
    high = a.astype(BF16)
    return high, (a - high.astype(F32)).astype(BF16)


def dot_split_left(a, b, ca, cb):
    high, low = split(a)
    return dot(high, b, ca, cb) + dot(low, b, ca, cb)


def dot_split_right(a, b, ca, cb):
    high, low = split(b)
    return dot(a, high, ca, cb) + dot(a, low, ca, cb)


def dot_split_both(a, b, ca, cb):
    a_high, a_low = split(a)
    b_high, b_low = split(b)
    return dot(a_high, b_high, ca, cb) + (dot(a_high, b_low, ca, cb) + dot(a_low, b_high, ca, cb))


def by_head(first, second, frames):
    lane = lax.broadcasted_iota(jnp.int32, (frames, PAIR), 1)
    return jnp.where(lane < HEAD_DIM, first, second)


def pair_column(cols, at, frames):
    return by_head(cols[:, at : at + 1], cols[:, 4 + at : 5 + at], frames)


def pair_weights(cols, rows, e, frames, later_rows):
    f_col, b_col = cols[:, 4 * e : 4 * e + 1], cols[:, 4 * e + 1 : 4 * e + 2]
    f_row, b_row = rows[4 * e : 4 * e + 1, :], rows[4 * e + 1 : 4 * e + 2, :]
    i = lax.broadcasted_iota(jnp.int32, (frames, frames), 0)
    j = lax.broadcasted_iota(jnp.int32, (frames, frames), 1)
    if later_rows:
        power = jnp.where(i >= j, f_col - f_row, b_row - b_col)
    else:
        power = jnp.where(j >= i, f_row - f_col, b_col - b_row)
    weight = jnp.exp(power)
    return jnp.where(i == j, 2.0 * weight, weight)


def pick(refs):
    part = pl.program_id(0) // (pl.num_programs(0) // len(refs))
    value = refs[0][...]
    for r in range(1, len(refs)):
        value = jnp.where(part == r, refs[r][...], value)
    return value


def put(refs, up, down):
    part = pl.program_id(0) // (pl.num_programs(0) // len(refs))
    for r, ref in enumerate(refs):
        @pl.when(part == r)
        def _():
            ref[0] = up
            ref[1] = down


def state_kernel(order_ref, x_ref, b_ref, cols_ref, *out_refs):
    frames = x_ref.shape[0]
    cols = cols_ref[0]
    x = x_ref[...].astype(F32)
    tail = jnp.exp(pair_column(cols, 2, frames))
    lead = jnp.exp(pair_column(cols, 1, frames))
    put(out_refs, dot_split_left(x * tail, b_ref[...], 0, 0),
        dot_split_left(x * lead, b_ref[...], 0, 0))


def within_kernel(order_ref, x_ref, b_ref, c_ref, cols_ref, rows_ref, w_ref, d_ref, gain_ref, skip_ref,
                  y_ref, m_ref, scores):
    frames = x_ref.shape[0]

    @pl.when(pl.program_id(0) == 0)
    def _():
        scores[...] = dot(c_ref[...], b_ref[...], 1, 1)

    cols, rows = cols_ref[0], rows_ref[0]
    x = x_ref[...]
    parts = []
    for e in range(2):
        pw = pair_weights(cols, rows, e, frames, True) * scores[...]
        parts.append(dot_split_left(pw, x, 1, 0))
    y_ref[...] = by_head(parts[0], parts[1], frames) + skip_ref[...] * x.astype(F32)
    m_ref[...] = dot(d_ref[...], w_ref[...], 1, 1) * gain_ref[...]


def merge_kernel(quad, order_ref, near_ref, m_ref, z_ref, c_ref, cols_ref, *refs):
    entry = pick(refs[:quad])
    y_ref, sums_ref, sq, cross = refs[quad:]
    frames = near_ref.shape[0]
    step = pl.program_id(0)

    @pl.when(step == 0)
    def _():
        sq[...] = jnp.zeros_like(sq)
        cross[...] = jnp.zeros_like(cross)

    cols = cols_ref[0]
    c = c_ref[...]
    y = near_ref[...]
    y = y + jnp.exp(pair_column(cols, 0, frames)) * dot_split_right(c, entry[0], 1, 1)
    y = y + jnp.exp(pair_column(cols, 3, frames)) * dot_split_right(c, entry[1], 1, 1)
    y_ref[...] = y
    z = z_ref[...].astype(F32)
    u = y * z * (1.0 / (1.0 + jnp.exp(-z)))
    sq[...] += u * u
    cross[...] += u * m_ref[...]

    @pl.when(step == pl.num_programs(0) - 1)
    def _():
        sums_ref[:, 0:1] = jnp.sum(sq[...], axis=1, keepdims=True)
        sums_ref[:, 1:2] = jnp.sum(cross[...], axis=1, keepdims=True)


def turn_kernel(inner, quad, order_ref, y_ref, m_ref, z_ref, c_ref, cols_ref, sums_ref, gain_ref,
                d_ref, dy_ref, gz_ref, *refs):
    back_refs, w_refs = refs[:quad], refs[quad:]
    frames = y_ref.shape[0]
    cols = cols_ref[0]
    y = y_ref[...]
    z = z_ref[...].astype(F32)
    sig = 1.0 / (1.0 + jnp.exp(-z))
    silu = z * sig
    u = y * silu
    q = lax.rsqrt(sums_ref[:, 0:1] * (1.0 / inner) + eps_norm)
    k = sums_ref[:, 1:2] * (1.0 / inner)
    du = q * m_ref[...] - u * (q * q * q * k)
    dy = du * silu
    dy_ref[...] = dy
    gz_ref[...] = (du * y * sig * (1.0 + z * (1.0 - sig))).astype(BF16)
    n = (u * q * gain_ref[...]).astype(BF16)
    c = c_ref[...]
    put(back_refs, dot_split_left(dy * jnp.exp(pair_column(cols, 3, frames)), c, 0, 0),
        dot_split_left(dy * jnp.exp(pair_column(cols, 0, frames)), c, 0, 0))
    at = 0
    for w_ref in w_refs:
        columns = w_ref.shape[1]
        w_ref[...] = dot(n, d_ref[:, at : at + columns], 0, 0) * weight_scale
        at += columns


def near_kernel(quad, order_ref, x_ref, b_ref, c_ref, cols_ref, rows_ref, skip_ref, dy_ref, *refs):
    entry = pick(refs[:quad])
    gx_ref, gb_ref, gc_ref, scores, pairs = refs[quad:]
    frames = x_ref.shape[0]
    step = pl.program_id(0)

    @pl.when(step == 0)
    def _():
        scores[...] = dot(b_ref[...], c_ref[...], 1, 1)
        pairs[...] = jnp.zeros_like(pairs)
        gc_ref[...] = jnp.zeros_like(gc_ref)

    cols, rows = cols_ref[0], rows_ref[0]
    x = x_ref[...]
    dy = dy_ref[...]
    lane = lax.broadcasted_iota(jnp.int32, (frames, PAIR), 1)
    parts = []
    for e in range(2):
        weight = pair_weights(cols, rows, e, frames, False)
        own = (lane < HEAD_DIM) if e == 0 else (lane >= HEAD_DIM)
        dy_own = jnp.where(own, dy, 0.0)
        pairs[...] += weight * dot_split_right(x, dy_own, 1, 1)
        parts.append(dot_split_both(weight * scores[...], dy_own, 1, 0))
    gx_ref[...] = parts[0] + parts[1] + skip_ref[...] * dy
    gc_ref[...] += dot_split_both(dy * jnp.exp(pair_column(cols, 0, frames)), entry[0], 1, 0)
    gc_ref[...] += dot_split_both(dy * jnp.exp(pair_column(cols, 3, frames)), entry[1], 1, 0)

    @pl.when(step == pl.num_programs(0) - 1)
    def _():
        gb_ref[...] = dot_split_left(pairs[...], c_ref[...], 1, 0)
        gc_ref[...] += dot_split_left(pairs[...], b_ref[...], 0, 0)


def far_kernel(quad, order_ref, x_ref, b_ref, cols_ref, near_ref, gb_near_ref, *refs):
    leave = pick(refs[:quad])
    gx_ref, gb_ref = refs[quad:]
    frames = x_ref.shape[0]

    @pl.when(pl.program_id(0) == 0)
    def _():
        gb_ref[...] = gb_near_ref[...]

    cols = cols_ref[0]
    b = b_ref[...]
    x = x_ref[...].astype(F32)
    tail = jnp.exp(pair_column(cols, 2, frames))
    lead = jnp.exp(pair_column(cols, 1, frames))
    far = tail * dot_split_right(b, leave[1], 1, 1) + lead * dot_split_right(b, leave[0], 1, 1)
    gx_ref[...] = (near_ref[...] + far).astype(BF16)
    gb_ref[...] += dot_split_both(x * tail, leave[1], 1, 0)
    gb_ref[...] += dot_split_both(x * lead, leave[0], 1, 0)


def call(kernel, name, order, ins, in_specs, outs, out_specs, scratch=(), flops=0):
    moved = sum(a.size * a.dtype.itemsize for a in ins) + sum(
        o.size * o.dtype.itemsize for o in outs)
    return pl.pallas_call(
        kernel,
        name=name,
        grid_spec=pltpu.PrefetchScalarGridSpec(
            num_scalar_prefetch=1,
            grid=(order.shape[0],),
            in_specs=in_specs,
            out_specs=out_specs,
            scratch_shapes=list(scratch),
        ),
        out_shape=outs,
        compiler_params=pltpu.CompilerParams(
            dimension_semantics=("arbitrary",), vmem_limit_bytes=VMEM_BYTES),
        cost_estimate=pl.CostEstimate(flops=flops, bytes_accessed=moved, transcendentals=0),
    )(order, *ins)


def small_call(kernel, name, factors, ins, outs):
    moved = sum(a.size * 4 for a in ins) + sum(o.size * 4 for o in outs)
    vmem = pl.BlockSpec(memory_space=pltpu.VMEM)
    return pl.pallas_call(
        kernel,
        name=name,
        in_specs=[pl.BlockSpec(memory_space=pltpu.SMEM)] + [vmem] * len(ins),
        out_specs=[vmem] * len(outs),
        out_shape=outs,
        compiler_params=pltpu.CompilerParams(vmem_limit_bytes=VMEM_BYTES),
        cost_estimate=pl.CostEstimate(flops=0, bytes_accessed=moved, transcendentals=0),
    )(factors, *ins)


def sum_over(value, axis):
    size = lax.axis_size(axis)
    reach = 1
    while reach < size:
        value = value + lax.ppermute(value, axis, [(i, i ^ reach) for i in range(size)])
        reach *= 2
    return value


def sum_slabs(value, bits):
    size, me = lax.axis_size("seq"), lax.axis_index("seq")
    for bit in bits:
        mine = (me >> bit) & 1
        halves = value.reshape(2, value.shape[0] // 2, value.shape[1])
        sent = lax.dynamic_index_in_dim(halves, 1 - mine, 0, keepdims=False)
        came = lax.ppermute(sent, "seq", [(i, i ^ (1 << bit)) for i in range(size)])
        value = lax.dynamic_index_in_dim(halves, mine, 0, keepdims=False) + came
    for bit in reversed(bits):
        mine = (me >> bit) & 1
        came = lax.ppermute(value, "seq", [(i, i ^ (1 << bit)) for i in range(size)])
        first = jnp.where(mine == 0, value, came)
        second = jnp.where(mine == 0, came, value)
        value = jnp.concatenate([first, second], axis=0)
    return value


def factor_reader(factors_ref, quad, heads, steps):
    kinds = 1 + 2 * quad + quad * quad + steps

    def read(d, kind, h):
        return factors_ref[(d * kinds + kind) * heads + h]

    return read


def total_kernel(quad, heads, steps, factors_ref, *refs):
    read = factor_reader(factors_ref, quad, heads, steps)
    for d in range(2):
        for h in range(heads):
            at = slice(h * HEAD_DIM, (h + 1) * HEAD_DIM)
            total = read(d, 0, h) * refs[0][d, at, :]
            for r in range(1, quad):
                total = total + read(d, r, h) * refs[r][d, at, :]
            refs[quad + d][at, :] = total


def advance_kernel(quad, heads, steps, k, factors_ref, *refs):
    read = factor_reader(factors_ref, quad, heads, steps)
    totals, came, before, sent, after = refs[:2], refs[2:4], refs[4:-4], refs[-4:-2], refs[-2:]
    for d in range(2):
        for h in range(heads):
            at = slice(h * HEAD_DIM, (h + 1) * HEAD_DIM)
            entering = came[d][at, :]
            if k:
                passed = read(d, 1 + 2 * quad + quad * quad + k, h)
                entering = before[d][at, :] + passed * entering
            after[d][at, :] = entering
            sent[d][at, :] = totals[d][at, :] + read(d, quad, h) * entering


def reply_kernel(quad, heads, steps, factors_ref, *refs):
    read = factor_reader(factors_ref, quad, heads, steps)
    held, came, before, replies = refs[:quad], refs[quad : quad + 2], refs[quad + 2 : -quad], refs[-quad:]
    k = steps - 1
    for d in range(2):
        for h in range(heads):
            at = slice(h * HEAD_DIM, (h + 1) * HEAD_DIM)
            entering = came[d][at, :]
            if k:
                passed = read(d, 1 + 2 * quad + quad * quad + k, h)
                entering = before[d][at, :] + passed * entering
            states = [held[s][d, at, :] for s in range(quad)]
            for r in range(quad):
                reply = read(d, quad + 1 + r, h) * entering
                for s in range(quad):
                    if s != r:
                        reply = reply + read(d, 1 + 2 * quad + s * quad + r, h) * states[s]
                replies[r][d, at, :] = reply


def scan_factors(ends_f, ends_b, quad, steps):
    size, me = lax.axis_size("seq"), lax.axis_index("seq")
    heads = ends_f.shape[0]
    table = jnp.concatenate([ends_f, ends_b])[None, :]
    reach = 1
    while reach < size:
        came = lax.ppermute(table, "seq", [(i, i ^ reach) for i in range(size)])
        table = jnp.concatenate([table, came], axis=0)
        reach *= 2
    none = -1
    runs = [(r, 0, none, quad) for r in range(quad)]
    runs += [(none, -1, none, quad)]
    runs += [(none, -1, r, 0) for r in range(quad)]
    runs += [(s, 0, r, 0) for s in range(quad) for r in range(quad)]
    runs += [(none, -(2 ** k - 1) * quad - 1, none, 0) for k in range(steps)]
    low_xor, low_add, high_xor, high_add = (jnp.array(v, jnp.int32) for v in zip(*runs))
    place = jnp.stack([me, size - 1 - me])[:, None]
    base = place // quad * quad
    low = jnp.where(low_xor == none, base + low_add, place ^ low_xor)
    high = jnp.where(high_xor == none, base + high_add, place ^ high_xor)
    slab = (place ^ jnp.arange(size, dtype=jnp.int32))[:, None, :]
    inside = (slab > low[:, :, None]) & (slab < high[:, :, None])
    logs = table.reshape(1, 1, size, 2 * heads)
    powers = jnp.sum(jnp.where(inside[..., None], logs, 0.0), axis=2)
    factors = jnp.where((low < high)[..., None], jnp.exp(powers), 0.0)
    return factors.reshape(2, len(runs), 2, heads)


def carry(mine, factors, quad, steps):
    size = lax.axis_size("seq")
    _, rows, width = mine[0].shape
    heads = rows // HEAD_DIM
    both = jax.ShapeDtypeStruct((2, rows, width), F32)
    one = jax.ShapeDtypeStruct((rows, width), F32)
    sizes = (quad, heads, steps)

    def trade(parts):
        return [parts[0]] + [
            lax.ppermute(parts[r], "seq", [(i, i ^ r) for i in range(size)])
            for r in range(1, quad)]

    held = trade(mine)
    totals = small_call(
        functools.partial(total_kernel, *sizes), "group_totals", factors, held, [one, one])
    sent, before = totals, []
    for k in range(steps):
        came = []
        for d, sign in enumerate((1, -1)):
            shift = sign * quad * 2 ** k
            came.append(lax.ppermute(
                sent[d], "seq", [(i, i + shift) for i in range(size) if 0 <= i + shift < size]))
        if k < steps - 1:
            new = small_call(
                functools.partial(advance_kernel, *sizes, k), "advance_scan", factors,
                [*totals, *came, *before], [one] * 4)
            sent, before = new[:2], new[2:]
    replies = small_call(
        functools.partial(reply_kernel, *sizes), "group_replies", factors,
        [*held, *came, *before], [both] * quad)
    return trade(replies)


def body(x_in, gate_in, b_in, c_in, decay_fwd, decay_bwd, skip_gain, norm_gain, w_out, d_out):
    frames, width = x_in.shape
    heads = decay_fwd.shape[0]
    state = b_in.shape[1]
    model = d_out.shape[1]
    pairs = heads // 2
    inner = width * lax.axis_size("head")

    fwd = jnp.cumsum(decay_fwd, axis=1)
    bwd = jnp.cumsum(decay_bwd, axis=1) - decay_bwd
    fwd_end = fwd[:, -1:]
    bwd_end = bwd[:, -1:] + decay_bwd[:, -1:]
    lines = jnp.stack([fwd, bwd, fwd_end - fwd, bwd_end - bwd], axis=1)
    rows = lines.reshape(pairs, 8, frames)
    cols = rows.transpose(0, 2, 1)
    quad = min(QUAD, pairs)
    per_part = pairs // quad
    part_heads = heads // quad
    slabs = lax.axis_size("seq")
    steps = (slabs // quad - 1).bit_length()
    q = lax.axis_index("seq") % quad
    turn = jnp.arange(pairs, dtype=jnp.int32)
    order = ((turn // per_part) ^ q) * per_part + turn % per_part
    factors = scan_factors(fwd_end[:, 0], bwd_end[:, 0], quad, steps)
    factors = lax.dynamic_slice_in_dim(factors, q * part_heads, part_heads, 3)
    entry_factors = jnp.stack([factors[0, :, 0], factors[1, :, 1]]).reshape(-1)
    exit_factors = jnp.stack([factors[0, :, 1], factors[1, :, 0]]).reshape(-1)
    skip = jnp.repeat(skip_gain, HEAD_DIM)[None, :]
    gain = norm_gain[None, :]

    wide = pl.BlockSpec((frames, PAIR), lambda i, p: (0, p[i]))
    narrow = pl.BlockSpec((frames, state), lambda i, p: (0, 0))
    col = pl.BlockSpec((1, frames, 8), lambda i, p: (p[i], 0, 0))
    row = pl.BlockSpec((1, 8, frames), lambda i, p: (p[i], 0, 0))
    lanes = pl.BlockSpec((1, PAIR), lambda i, p: (0, p[i]))
    states = [
        pl.BlockSpec((2, PAIR, state),
                     lambda i, p, r=r: (0, jnp.clip(i - r * per_part, 0, per_part - 1), 0))
        for r in range(quad)]
    model_rows = pl.BlockSpec((frames, model), lambda i, p: (0, 0))
    weight_rows = pl.BlockSpec((PAIR, model), lambda i, p: (p[i], 0))
    sums_spec = pl.BlockSpec((frames, 2), lambda i, p: (0, 0))
    shape = jax.ShapeDtypeStruct
    wide_f32, wide_bf16 = shape((frames, width), F32), shape((frames, width), BF16)
    state_out = [shape((2, width // quad, state), F32)] * quad
    narrow_out = shape((frames, state), F32)
    square = pltpu.VMEM((frames, frames), F32)
    lane_sums = pltpu.VMEM((frames, PAIR), F32)
    quad_flops = 2 * frames * frames * width

    local = call(state_kernel, "local_states", order, (x_in, b_in, cols), [wide, narrow, col],
                 state_out, states, flops=8 * frames * width * state)
    entry = carry(local, entry_factors, quad, steps)
    near_y, scaled = call(
        within_kernel, "within_slab", order,
        (x_in, b_in, c_in, cols, rows, w_out, d_out, gain, skip),
        [wide, narrow, narrow, col, row, weight_rows, model_rows, lanes, lanes],
        [wide_f32, wide_f32], [wide, wide], [square],
        flops=8 * quad_flops + 2 * frames * width * model)
    y, sums = call(
        functools.partial(merge_kernel, quad), "merge_entry", order,
        (near_y, scaled, gate_in, c_in, cols, *entry),
        [wide, wide, wide, narrow, col, *states],
        [wide_f32, shape((frames, 2), F32)], [wide, sums_spec], [lane_sums, lane_sums],
        flops=8 * frames * width * state)
    sums = sum_over(sums, "head")
    bits = list(range((lax.axis_size("seq") - 1).bit_length()))
    orders = (bits, [bits[1], bits[0]] + bits[2:], bits[2:] + bits[:2])
    thirds = model // 8 * 3
    chunks = (thirds, thirds, model - 2 * thirds)
    dy, grad_z, *rest = call(
        functools.partial(turn_kernel, inner, quad), "norm_backward", order,
        (y, scaled, gate_in, c_in, cols, sums, gain, d_out),
        [wide, wide, wide, narrow, col, sums_spec, lanes, model_rows],
        [wide_f32, wide_bf16, *state_out] + [shape((width, n), F32) for n in chunks],
        [wide, wide, *states] + [pl.BlockSpec((PAIR, n), lambda i, p: (p[i], 0)) for n in chunks],
        flops=2 * frames * width * model + 8 * frames * width * state)
    back, local_w = rest[:quad], rest[quad:]
    exits = carry(back, exit_factors, quad, steps)
    grad_w = jnp.concatenate(
        [sum_slabs(part, order) for part, order in zip(local_w, orders)], axis=1)
    near_x, near_b, grad_c = call(
        functools.partial(near_kernel, quad), "near_gradients", order,
        (x_in, b_in, c_in, cols, rows, skip, dy, *entry),
        [wide, narrow, narrow, col, row, lanes, wide, *states],
        [wide_f32, narrow_out, narrow_out], [wide, narrow, narrow], [square, square],
        flops=20 * quad_flops)
    grad_c = sum_over(grad_c, "head")
    grad_x, grad_b = call(
        functools.partial(far_kernel, quad), "far_gradients", order,
        (x_in, b_in, cols, near_x, near_b, *exits),
        [wide, narrow, col, wide, narrow, *states],
        [wide_bf16, narrow_out], [wide, narrow], flops=20 * frames * width * state)
    grad_b = sum_over(grad_b, "head")
    return grad_x, grad_z, grad_b, grad_c, grad_w


def solution(mesh):
    in_specs = (
        P("seq", "head"),
        P("seq", "head"),
        P("seq", None),
        P("seq", None),
        P("head", "seq"),
        P("head", "seq"),
        P("head"),
        P("head"),
        P("head", None),
        P("seq", None),
    )
    out_specs = (
        P("seq", "head"),
        P("seq", "head"),
        P("seq", None),
        P("seq", None),
        P("head", None),
    )
    return jax.shard_map(body, mesh=mesh, in_specs=in_specs, out_specs=out_specs, check_vma=False)
```

```python
import functools

import jax
import jax.numpy as jnp
from jax import lax
from jax.experimental import pallas as pl
from jax.experimental.pallas import tpu as pltpu
from jax.sharding import PartitionSpec as P

HEAD_DIM = 64
PAIR = 2 * HEAD_DIM
QUAD = 4
F32 = jnp.float32
BF16 = jnp.bfloat16
eps_norm = 1e-05
weight_scale = 0.0078125
VMEM_BYTES = 48 * 1024 * 1024


def dot(a, b, ca, cb):
    return lax.dot_general(a, b, (((ca,), (cb,)), ((), ())), preferred_element_type=F32)


def split(a):
    high = a.astype(BF16)
    return high, (a - high.astype(F32)).astype(BF16)


def dot_split_left(a, b, ca, cb):
    high, low = split(a)
    return dot(high, b, ca, cb) + dot(low, b, ca, cb)


def dot_split_right(a, b, ca, cb):
    high, low = split(b)
    return dot(a, high, ca, cb) + dot(a, low, ca, cb)


def dot_split_both(a, b, ca, cb):
    a_high, a_low = split(a)
    b_high, b_low = split(b)
    return dot(a_high, b_high, ca, cb) + (dot(a_high, b_low, ca, cb) + dot(a_low, b_high, ca, cb))


def by_head(first, second, frames):
    lane = lax.broadcasted_iota(jnp.int32, (frames, PAIR), 1)
    return jnp.where(lane < HEAD_DIM, first, second)


def pair_column(cols, at, frames):
    return by_head(cols[:, at : at + 1], cols[:, 4 + at : 5 + at], frames)


def pair_weights(cols, rows, e, frames, later_rows):
    f_col, b_col = cols[:, 4 * e : 4 * e + 1], cols[:, 4 * e + 1 : 4 * e + 2]
    f_row, b_row = rows[4 * e : 4 * e + 1, :], rows[4 * e + 1 : 4 * e + 2, :]
    i = lax.broadcasted_iota(jnp.int32, (frames, frames), 0)
    j = lax.broadcasted_iota(jnp.int32, (frames, frames), 1)
    if later_rows:
        power = jnp.where(i >= j, f_col - f_row, b_row - b_col)
    else:
        power = jnp.where(j >= i, f_row - f_col, b_col - b_row)
    weight = jnp.exp(power)
    return jnp.where(i == j, 2.0 * weight, weight)


def pick(refs):
    part = pl.program_id(0) // (pl.num_programs(0) // len(refs))
    value = refs[0][...]
    for r in range(1, len(refs)):
        value = jnp.where(part == r, refs[r][...], value)
    return value


def put(refs, up, down):
    part = pl.program_id(0) // (pl.num_programs(0) // len(refs))
    for r, ref in enumerate(refs):
        @pl.when(part == r)
        def _():
            ref[0] = up
            ref[1] = down


def state_kernel(order_ref, x_ref, b_ref, cols_ref, *out_refs):
    frames = x_ref.shape[0]
    cols = cols_ref[0]
    x = x_ref[...].astype(F32)
    tail = jnp.exp(pair_column(cols, 2, frames))
    lead = jnp.exp(pair_column(cols, 1, frames))
    put(out_refs, dot_split_left(x * tail, b_ref[...], 0, 0),
        dot_split_left(x * lead, b_ref[...], 0, 0))


def within_kernel(order_ref, x_ref, b_ref, c_ref, cols_ref, rows_ref, w_ref, d_ref, gain_ref, skip_ref,
                  y_ref, m_ref, scores):
    frames = x_ref.shape[0]

    @pl.when(pl.program_id(0) == 0)
    def _():
        scores[...] = dot(c_ref[...], b_ref[...], 1, 1)

    cols, rows = cols_ref[0], rows_ref[0]
    x = x_ref[...]
    parts = []
    for e in range(2):
        pw = pair_weights(cols, rows, e, frames, True) * scores[...]
        parts.append(dot_split_left(pw, x, 1, 0))
    y_ref[...] = by_head(parts[0], parts[1], frames) + skip_ref[...] * x.astype(F32)
    m_ref[...] = dot(d_ref[...], w_ref[...], 1, 1) * gain_ref[...]


def merge_kernel(quad, order_ref, near_ref, m_ref, z_ref, c_ref, cols_ref, *refs):
    entry = pick(refs[:quad])
    y_ref, sums_ref, sq, cross = refs[quad:]
    frames = near_ref.shape[0]
    step = pl.program_id(0)

    @pl.when(step == 0)
    def _():
        sq[...] = jnp.zeros_like(sq)
        cross[...] = jnp.zeros_like(cross)

    cols = cols_ref[0]
    c = c_ref[...]
    y = near_ref[...]
    y = y + jnp.exp(pair_column(cols, 0, frames)) * dot_split_right(c, entry[0], 1, 1)
    y = y + jnp.exp(pair_column(cols, 3, frames)) * dot_split_right(c, entry[1], 1, 1)
    y_ref[...] = y
    z = z_ref[...].astype(F32)
    u = y * z * (1.0 / (1.0 + jnp.exp(-z)))
    sq[...] += u * u
    cross[...] += u * m_ref[...]

    @pl.when(step == pl.num_programs(0) - 1)
    def _():
        sums_ref[:, 0:1] = jnp.sum(sq[...], axis=1, keepdims=True)
        sums_ref[:, 1:2] = jnp.sum(cross[...], axis=1, keepdims=True)


def turn_kernel(inner, quad, order_ref, y_ref, m_ref, z_ref, c_ref, cols_ref, sums_ref, gain_ref,
                d_ref, dy_ref, gz_ref, *refs):
    back_refs, w_refs = refs[:quad], refs[quad:]
    frames = y_ref.shape[0]
    cols = cols_ref[0]
    y = y_ref[...]
    z = z_ref[...].astype(F32)
    sig = 1.0 / (1.0 + jnp.exp(-z))
    silu = z * sig
    u = y * silu
    q = lax.rsqrt(sums_ref[:, 0:1] * (1.0 / inner) + eps_norm)
    k = sums_ref[:, 1:2] * (1.0 / inner)
    du = q * m_ref[...] - u * (q * q * q * k)
    dy = du * silu
    dy_ref[...] = dy
    gz_ref[...] = (du * y * sig * (1.0 + z * (1.0 - sig))).astype(BF16)
    n = (u * q * gain_ref[...]).astype(BF16)
    c = c_ref[...]
    put(back_refs, dot_split_left(dy * jnp.exp(pair_column(cols, 3, frames)), c, 0, 0),
        dot_split_left(dy * jnp.exp(pair_column(cols, 0, frames)), c, 0, 0))
    at = 0
    for w_ref in w_refs:
        columns = w_ref.shape[1]
        w_ref[...] = dot(n, d_ref[:, at : at + columns], 0, 0) * weight_scale
        at += columns


def near_kernel(quad, order_ref, x_ref, b_ref, c_ref, cols_ref, rows_ref, skip_ref, dy_ref, *refs):
    entry = pick(refs[:quad])
    gx_ref, gb_ref, gc_ref, scores, pairs = refs[quad:]
    frames = x_ref.shape[0]
    step = pl.program_id(0)

    @pl.when(step == 0)
    def _():
        scores[...] = dot(b_ref[...], c_ref[...], 1, 1)
        pairs[...] = jnp.zeros_like(pairs)
        gc_ref[...] = jnp.zeros_like(gc_ref)

    cols, rows = cols_ref[0], rows_ref[0]
    x = x_ref[...]
    dy = dy_ref[...]
    lane = lax.broadcasted_iota(jnp.int32, (frames, PAIR), 1)
    parts = []
    for e in range(2):
        weight = pair_weights(cols, rows, e, frames, False)
        own = (lane < HEAD_DIM) if e == 0 else (lane >= HEAD_DIM)
        dy_own = jnp.where(own, dy, 0.0)
        pairs[...] += weight * dot_split_right(x, dy_own, 1, 1)
        parts.append(dot_split_both(weight * scores[...], dy_own, 1, 0))
    gx_ref[...] = parts[0] + parts[1] + skip_ref[...] * dy
    gc_ref[...] += dot_split_both(dy * jnp.exp(pair_column(cols, 0, frames)), entry[0], 1, 0)
    gc_ref[...] += dot_split_both(dy * jnp.exp(pair_column(cols, 3, frames)), entry[1], 1, 0)

    @pl.when(step == pl.num_programs(0) - 1)
    def _():
        gb_ref[...] = dot_split_left(pairs[...], c_ref[...], 1, 0)
        gc_ref[...] += dot_split_left(pairs[...], b_ref[...], 0, 0)


def far_kernel(quad, order_ref, x_ref, b_ref, cols_ref, near_ref, gb_near_ref, *refs):
    leave = pick(refs[:quad])
    gx_ref, gb_ref = refs[quad:]
    frames = x_ref.shape[0]

    @pl.when(pl.program_id(0) == 0)
    def _():
        gb_ref[...] = gb_near_ref[...]

    cols = cols_ref[0]
    b = b_ref[...]
    x = x_ref[...].astype(F32)
    tail = jnp.exp(pair_column(cols, 2, frames))
    lead = jnp.exp(pair_column(cols, 1, frames))
    far = tail * dot_split_right(b, leave[1], 1, 1) + lead * dot_split_right(b, leave[0], 1, 1)
    gx_ref[...] = (near_ref[...] + far).astype(BF16)
    gb_ref[...] += dot_split_both(x * tail, leave[1], 1, 0)
    gb_ref[...] += dot_split_both(x * lead, leave[0], 1, 0)


def call(kernel, name, order, ins, in_specs, outs, out_specs, scratch=(), flops=0):
    moved = sum(a.size * a.dtype.itemsize for a in ins) + sum(
        o.size * o.dtype.itemsize for o in outs)
    return pl.pallas_call(
        kernel,
        name=name,
        grid_spec=pltpu.PrefetchScalarGridSpec(
            num_scalar_prefetch=1,
            grid=(order.shape[0],),
            in_specs=in_specs,
            out_specs=out_specs,
            scratch_shapes=list(scratch),
        ),
        out_shape=outs,
        compiler_params=pltpu.CompilerParams(
            dimension_semantics=("arbitrary",), vmem_limit_bytes=VMEM_BYTES),
        cost_estimate=pl.CostEstimate(flops=flops, bytes_accessed=moved, transcendentals=0),
    )(order, *ins)


def small_call(kernel, name, factors, ins, outs):
    moved = sum(a.size * 4 for a in ins) + sum(o.size * 4 for o in outs)
    vmem = pl.BlockSpec(memory_space=pltpu.VMEM)
    return pl.pallas_call(
        kernel,
        name=name,
        in_specs=[pl.BlockSpec(memory_space=pltpu.SMEM)] + [vmem] * len(ins),
        out_specs=[vmem] * len(outs),
        out_shape=outs,
        compiler_params=pltpu.CompilerParams(vmem_limit_bytes=VMEM_BYTES),
        cost_estimate=pl.CostEstimate(flops=0, bytes_accessed=moved, transcendentals=0),
    )(factors, *ins)


def sum_over(value, axis):
    size = lax.axis_size(axis)
    reach = 1
    while reach < size:
        value = value + lax.ppermute(value, axis, [(i, i ^ reach) for i in range(size)])
        reach *= 2
    return value


def exchange(value, bit):
    size = lax.axis_size("seq")
    return lax.ppermute(value, "seq", [(i, i ^ (1 << bit)) for i in range(size)])


def sum_slabs(values, orders, beside):
    me = lax.axis_index("seq")
    count = len(orders[0])
    values = list(values)
    for n in range(count):
        kept, came = [], []
        for value, bits in zip(values, orders):
            mine = (me >> bits[n]) & 1
            halves = value.reshape(2, value.shape[0] // 2, value.shape[1])
            kept.append(lax.dynamic_index_in_dim(halves, mine, 0, keepdims=False))
            came.append(exchange(
                lax.dynamic_index_in_dim(halves, 1 - mine, 0, keepdims=False), bits[n]))
        came = beside(n, came)
        values = [a + b for a, b in zip(kept, came)]
    for n in reversed(range(count)):
        came = [exchange(value, bits[n]) for value, bits in zip(values, orders)]
        came = beside(2 * count - 1 - n, came)
        for i, (other, bits) in enumerate(zip(came, orders)):
            first = ((me >> bits[n]) & 1) == 0
            values[i] = jnp.concatenate(
                [jnp.where(first, values[i], other), jnp.where(first, other, values[i])], axis=0)
    return jnp.concatenate(values, axis=1)


def factor_reader(factors_ref, quad, heads, steps):
    kinds = 1 + 2 * quad + quad * quad + steps

    def read(d, kind, h):
        return factors_ref[(d * kinds + kind) * heads + h]

    return read


def total_kernel(quad, heads, steps, factors_ref, *refs):
    read = factor_reader(factors_ref, quad, heads, steps)
    for d in range(2):
        for h in range(heads):
            at = slice(h * HEAD_DIM, (h + 1) * HEAD_DIM)
            total = read(d, 0, h) * refs[0][d, at, :]
            for r in range(1, quad):
                total = total + read(d, r, h) * refs[r][d, at, :]
            refs[quad + d][at, :] = total


def advance_kernel(quad, heads, steps, k, factors_ref, *refs):
    read = factor_reader(factors_ref, quad, heads, steps)
    totals, came, before, sent, after = refs[:2], refs[2:4], refs[4:-4], refs[-4:-2], refs[-2:]
    for d in range(2):
        for h in range(heads):
            at = slice(h * HEAD_DIM, (h + 1) * HEAD_DIM)
            entering = came[d][at, :]
            if k:
                passed = read(d, 1 + 2 * quad + quad * quad + k, h)
                entering = before[d][at, :] + passed * entering
            after[d][at, :] = entering
            sent[d][at, :] = totals[d][at, :] + read(d, quad, h) * entering


def reply_kernel(quad, heads, steps, factors_ref, *refs):
    read = factor_reader(factors_ref, quad, heads, steps)
    held, came, before, replies = refs[:quad], refs[quad : quad + 2], refs[quad + 2 : -quad], refs[-quad:]
    k = steps - 1
    for d in range(2):
        for h in range(heads):
            at = slice(h * HEAD_DIM, (h + 1) * HEAD_DIM)
            entering = came[d][at, :]
            if k:
                passed = read(d, 1 + 2 * quad + quad * quad + k, h)
                entering = before[d][at, :] + passed * entering
            states = [held[s][d, at, :] for s in range(quad)]
            for r in range(quad):
                reply = read(d, quad + 1 + r, h) * entering
                for s in range(quad):
                    if s != r:
                        reply = reply + read(d, 1 + 2 * quad + s * quad + r, h) * states[s]
                replies[r][d, at, :] = reply


def scan_factors(ends_f, ends_b, quad, steps):
    size, me = lax.axis_size("seq"), lax.axis_index("seq")
    heads = ends_f.shape[0]
    table = jnp.concatenate([ends_f, ends_b])[None, :]
    reach = 1
    while reach < size:
        came = lax.ppermute(table, "seq", [(i, i ^ reach) for i in range(size)])
        table = jnp.concatenate([table, came], axis=0)
        reach *= 2
    none = -1
    runs = [(r, 0, none, quad) for r in range(quad)]
    runs += [(none, -1, none, quad)]
    runs += [(none, -1, r, 0) for r in range(quad)]
    runs += [(s, 0, r, 0) for s in range(quad) for r in range(quad)]
    runs += [(none, -(2 ** k - 1) * quad - 1, none, 0) for k in range(steps)]
    low_xor, low_add, high_xor, high_add = (jnp.array(v, jnp.int32) for v in zip(*runs))
    place = jnp.stack([me, size - 1 - me])[:, None]
    base = place // quad * quad
    low = jnp.where(low_xor == none, base + low_add, place ^ low_xor)
    high = jnp.where(high_xor == none, base + high_add, place ^ high_xor)
    slab = (place ^ jnp.arange(size, dtype=jnp.int32))[:, None, :]
    inside = (slab > low[:, :, None]) & (slab < high[:, :, None])
    logs = table.reshape(1, 1, size, 2 * heads)
    powers = jnp.sum(jnp.where(inside[..., None], logs, 0.0), axis=2)
    factors = jnp.where((low < high)[..., None], jnp.exp(powers), 0.0)
    return factors.reshape(2, len(runs), 2, heads)


def carry(mine, factors, quad, steps):
    size = lax.axis_size("seq")
    _, rows, width = mine[0].shape
    heads = rows // HEAD_DIM
    both = jax.ShapeDtypeStruct((2, rows, width), F32)
    one = jax.ShapeDtypeStruct((rows, width), F32)
    sizes = (quad, heads, steps)

    def trade(parts):
        return [parts[0]] + [
            lax.ppermute(parts[r], "seq", [(i, i ^ r) for i in range(size)])
            for r in range(1, quad)]

    held = yield trade(mine)
    totals = small_call(
        functools.partial(total_kernel, *sizes), "group_totals", factors, held, [one, one])
    sent, before = totals, []
    for k in range(steps):
        came = []
        for d, sign in enumerate((1, -1)):
            shift = sign * quad * 2 ** k
            came.append(lax.ppermute(
                sent[d], "seq", [(i, i + shift) for i in range(size) if 0 <= i + shift < size]))
        came = yield came
        if k < steps - 1:
            new = small_call(
                functools.partial(advance_kernel, *sizes, k), "advance_scan", factors,
                [*totals, *came, *before], [one] * 4)
            sent, before = new[:2], new[2:]
    replies = small_call(
        functools.partial(reply_kernel, *sizes), "group_replies", factors,
        [*held, *came, *before], [both] * quad)
    return (yield trade(replies))


def body(x_in, gate_in, b_in, c_in, decay_fwd, decay_bwd, skip_gain, norm_gain, w_out, d_out):
    frames, width = x_in.shape
    heads = decay_fwd.shape[0]
    state = b_in.shape[1]
    model = d_out.shape[1]
    pairs = heads // 2
    inner = width * lax.axis_size("head")

    fwd = jnp.cumsum(decay_fwd, axis=1)
    bwd = jnp.cumsum(decay_bwd, axis=1) - decay_bwd
    fwd_end = fwd[:, -1:]
    bwd_end = bwd[:, -1:] + decay_bwd[:, -1:]
    lines = jnp.stack([fwd, bwd, fwd_end - fwd, bwd_end - bwd], axis=1)
    rows = lines.reshape(pairs, 8, frames)
    cols = rows.transpose(0, 2, 1)
    quad = min(QUAD, pairs)
    per_part = pairs // quad
    part_heads = heads // quad
    slabs = lax.axis_size("seq")
    steps = (slabs // quad - 1).bit_length()
    q = lax.axis_index("seq") % quad
    turn = jnp.arange(pairs, dtype=jnp.int32)
    order = ((turn // per_part) ^ q) * per_part + turn % per_part
    factors = scan_factors(fwd_end[:, 0], bwd_end[:, 0], quad, steps)
    factors = lax.dynamic_slice_in_dim(factors, q * part_heads, part_heads, 3)
    entry_factors = jnp.stack([factors[0, :, 0], factors[1, :, 1]]).reshape(-1)
    exit_factors = jnp.stack([factors[0, :, 1], factors[1, :, 0]]).reshape(-1)
    skip = jnp.repeat(skip_gain, HEAD_DIM)[None, :]
    gain = norm_gain[None, :]

    wide = pl.BlockSpec((frames, PAIR), lambda i, p: (0, p[i]))
    narrow = pl.BlockSpec((frames, state), lambda i, p: (0, 0))
    col = pl.BlockSpec((1, frames, 8), lambda i, p: (p[i], 0, 0))
    row = pl.BlockSpec((1, 8, frames), lambda i, p: (p[i], 0, 0))
    lanes = pl.BlockSpec((1, PAIR), lambda i, p: (0, p[i]))
    states = [
        pl.BlockSpec((2, PAIR, state),
                     lambda i, p, r=r: (0, jnp.clip(i - r * per_part, 0, per_part - 1), 0))
        for r in range(quad)]
    model_rows = pl.BlockSpec((frames, model), lambda i, p: (0, 0))
    weight_rows = pl.BlockSpec((PAIR, model), lambda i, p: (p[i], 0))
    sums_spec = pl.BlockSpec((frames, 2), lambda i, p: (0, 0))
    shape = jax.ShapeDtypeStruct
    wide_f32, wide_bf16 = shape((frames, width), F32), shape((frames, width), BF16)
    state_out = [shape((2, width // quad, state), F32)] * quad
    narrow_out = shape((frames, state), F32)
    square = pltpu.VMEM((frames, frames), F32)
    lane_sums = pltpu.VMEM((frames, PAIR), F32)
    quad_flops = 2 * frames * frames * width

    local = call(state_kernel, "local_states", order, (x_in, b_in, cols), [wide, narrow, col],
                 state_out, states, flops=8 * frames * width * state)
    near_y, scaled = call(
        within_kernel, "within_slab", order,
        (x_in, b_in, c_in, cols, rows, w_out, d_out, gain, skip),
        [wide, narrow, narrow, col, row, weight_rows, model_rows, lanes, lanes],
        [wide_f32, wide_f32], [wide, wide], [square],
        flops=8 * quad_flops + 2 * frames * width * model)
    stages = carry(local, entry_factors, quad, steps)
    flying, at = next(stages), 0
    while at <= steps:
        if at == 1:
            flying, near_y, scaled = lax.optimization_barrier((flying, near_y, scaled))
        flying, at = stages.send(flying), at + 1
    entry = flying
    y, sums = call(
        functools.partial(merge_kernel, quad), "merge_entry", order,
        (near_y, scaled, gate_in, c_in, cols, *entry),
        [wide, wide, wide, narrow, col, *states],
        [wide_f32, shape((frames, 2), F32)], [wide, sums_spec], [lane_sums, lane_sums],
        flops=8 * frames * width * state)
    sums = sum_over(sums, "head")
    bits = list(range((lax.axis_size("seq") - 1).bit_length()))
    orders = (bits, [bits[1], bits[0]] + bits[2:], bits[2:] + bits[:2])
    thirds = model // 8 * 3
    chunks = (thirds, thirds, model - 2 * thirds)
    dy, grad_z, *rest = call(
        functools.partial(turn_kernel, inner, quad), "norm_backward", order,
        (y, scaled, gate_in, c_in, cols, sums, gain, d_out),
        [wide, wide, wide, narrow, col, sums_spec, lanes, model_rows],
        [wide_f32, wide_bf16, *state_out] + [shape((width, n), F32) for n in chunks],
        [wide, wide, *states] + [pl.BlockSpec((PAIR, n), lambda i, p: (p[i], 0)) for n in chunks],
        flops=2 * frames * width * model + 8 * frames * width * state)
    back, local_w = rest[:quad], rest[quad:]
    stages = carry(back, exit_factors, quad, steps)
    near_x, near_b, grad_c = call(
        functools.partial(near_kernel, quad), "near_gradients", order,
        (x_in, b_in, c_in, cols, rows, skip, dy, *entry),
        [wide, narrow, narrow, col, row, lanes, wide, *states],
        [wide_f32, narrow_out, narrow_out], [wide, narrow, narrow], [square, square],
        flops=20 * quad_flops)
    held = {"near": (near_x, near_b, grad_c)}
    last = steps + 1

    def beside(n, came):
        stage = n - 2
        if n == 0:
            came, held["near"] = lax.optimization_barrier((came, held["near"]))
        elif n == 1:
            held["c"] = sum_over(held["near"][2], "head")
            came, held["c"] = lax.optimization_barrier((came, held["c"]))
        elif stage <= last:
            flying = held["next"] if stage else next(stages)
            came, flying = lax.optimization_barrier((came, flying))
            held["next"] = flying if stage == last else stages.send(flying)
        elif stage == last + 1:
            far = call(
                functools.partial(far_kernel, quad), "far_gradients", order,
                (x_in, b_in, cols, held["near"][0], held["near"][1], *held["next"]),
                [wide, narrow, col, wide, narrow, *states],
                [wide_bf16, narrow_out], [wide, narrow], flops=20 * frames * width * state)
            came, held["far"] = lax.optimization_barrier((came, far))
        elif stage == last + 2:
            held["b"] = sum_over(held["far"][1], "head")
            came, held["b"] = lax.optimization_barrier((came, held["b"]))
        return came

    grad_w = sum_slabs(local_w, orders, beside)
    return held["far"][0], grad_z, held["b"], held["c"], grad_w


def solution(mesh):
    in_specs = (
        P("seq", "head"),
        P("seq", "head"),
        P("seq", None),
        P("seq", None),
        P("head", "seq"),
        P("head", "seq"),
        P("head"),
        P("head"),
        P("head", None),
        P("seq", None),
    )
    out_specs = (
        P("seq", "head"),
        P("seq", "head"),
        P("seq", None),
        P("seq", None),
        P("head", None),
    )
    return jax.shard_map(body, mesh=mesh, in_specs=in_specs, out_specs=out_specs, check_vma=False)
```

```python
import functools

import jax
import jax.numpy as jnp
from jax import lax
from jax.experimental import pallas as pl
from jax.experimental.pallas import tpu as pltpu
from jax.sharding import PartitionSpec as P

HEAD_DIM = 64
PAIR = 2 * HEAD_DIM
QUAD = 4
F32 = jnp.float32
BF16 = jnp.bfloat16
eps_norm = 1e-05
weight_scale = 0.0078125
VMEM_BYTES = 48 * 1024 * 1024


def dot(a, b, ca, cb):
    return lax.dot_general(a, b, (((ca,), (cb,)), ((), ())), preferred_element_type=F32)


def split(a):
    high = a.astype(BF16)
    return high, (a - high.astype(F32)).astype(BF16)


def dot_split_left(a, b, ca, cb):
    high, low = split(a)
    return dot(high, b, ca, cb) + dot(low, b, ca, cb)


def dot_split_right(a, b, ca, cb):
    high, low = split(b)
    return dot(a, high, ca, cb) + dot(a, low, ca, cb)


def dot_split_both(a, b, ca, cb):
    a_high, a_low = split(a)
    b_high, b_low = split(b)
    return dot(a_high, b_high, ca, cb) + (dot(a_high, b_low, ca, cb) + dot(a_low, b_high, ca, cb))


def by_head(first, second, frames):
    lane = lax.broadcasted_iota(jnp.int32, (frames, PAIR), 1)
    return jnp.where(lane < HEAD_DIM, first, second)


def pair_column(cols, at, frames):
    return by_head(cols[:, at : at + 1], cols[:, 4 + at : 5 + at], frames)


def pair_weights(cols, rows, e, frames, later_rows):
    f_col, b_col = cols[:, 4 * e : 4 * e + 1], cols[:, 4 * e + 1 : 4 * e + 2]
    f_row, b_row = rows[4 * e : 4 * e + 1, :], rows[4 * e + 1 : 4 * e + 2, :]
    i = lax.broadcasted_iota(jnp.int32, (frames, frames), 0)
    j = lax.broadcasted_iota(jnp.int32, (frames, frames), 1)
    if later_rows:
        power = jnp.where(i >= j, f_col - f_row, b_row - b_col)
    else:
        power = jnp.where(j >= i, f_row - f_col, b_col - b_row)
    weight = jnp.exp(power)
    return jnp.where(i == j, 2.0 * weight, weight)


def pick(refs):
    part = pl.program_id(0) // (pl.num_programs(0) // len(refs))
    value = refs[0][...]
    for r in range(1, len(refs)):
        value = jnp.where(part == r, refs[r][...], value)
    return value


def put(refs, up, down):
    part = pl.program_id(0) // (pl.num_programs(0) // len(refs))
    for r, ref in enumerate(refs):
        @pl.when(part == r)
        def _():
            ref[0] = up
            ref[1] = down


def state_kernel(order_ref, x_ref, b_ref, cols_ref, *out_refs):
    frames = x_ref.shape[0]
    cols = cols_ref[0]
    x = x_ref[...].astype(F32)
    tail = jnp.exp(pair_column(cols, 2, frames))
    lead = jnp.exp(pair_column(cols, 1, frames))
    put(out_refs, dot_split_left(x * tail, b_ref[...], 0, 0),
        dot_split_left(x * lead, b_ref[...], 0, 0))


def within_kernel(order_ref, x_ref, b_ref, c_ref, cols_ref, rows_ref, w_ref, d_ref, gain_ref, skip_ref,
                  y_ref, m_ref, scores):
    frames = x_ref.shape[0]

    @pl.when(pl.program_id(0) == 0)
    def _():
        scores[...] = dot(c_ref[...], b_ref[...], 1, 1)

    cols, rows = cols_ref[0], rows_ref[0]
    x = x_ref[...]
    parts = []
    for e in range(2):
        pw = pair_weights(cols, rows, e, frames, True) * scores[...]
        parts.append(dot_split_left(pw, x, 1, 0))
    y_ref[...] = by_head(parts[0], parts[1], frames) + skip_ref[...] * x.astype(F32)
    m_ref[...] = dot(d_ref[...], w_ref[...], 1, 1) * gain_ref[...]


def merge_kernel(quad, order_ref, near_ref, m_ref, z_ref, c_ref, cols_ref, *refs):
    entry = pick(refs[:quad])
    y_ref, sums_ref, sq, cross = refs[quad:]
    frames = near_ref.shape[0]
    step = pl.program_id(0)

    @pl.when(step == 0)
    def _():
        sq[...] = jnp.zeros_like(sq)
        cross[...] = jnp.zeros_like(cross)

    cols = cols_ref[0]
    c = c_ref[...]
    y = near_ref[...]
    y = y + jnp.exp(pair_column(cols, 0, frames)) * dot_split_right(c, entry[0], 1, 1)
    y = y + jnp.exp(pair_column(cols, 3, frames)) * dot_split_right(c, entry[1], 1, 1)
    y_ref[...] = y
    z = z_ref[...].astype(F32)
    u = y * z * (1.0 / (1.0 + jnp.exp(-z)))
    sq[...] += u * u
    cross[...] += u * m_ref[...]

    @pl.when(step == pl.num_programs(0) - 1)
    def _():
        sums_ref[:, 0:1] = jnp.sum(sq[...], axis=1, keepdims=True)
        sums_ref[:, 1:2] = jnp.sum(cross[...], axis=1, keepdims=True)


def turn_kernel(inner, quad, order_ref, y_ref, m_ref, z_ref, c_ref, cols_ref, sums_ref, gain_ref,
                d_ref, dy_ref, gz_ref, *refs):
    back_refs, w_refs = refs[:quad], refs[quad:]
    frames = y_ref.shape[0]
    cols = cols_ref[0]
    y = y_ref[...]
    z = z_ref[...].astype(F32)
    sig = 1.0 / (1.0 + jnp.exp(-z))
    silu = z * sig
    u = y * silu
    q = lax.rsqrt(sums_ref[:, 0:1] * (1.0 / inner) + eps_norm)
    k = sums_ref[:, 1:2] * (1.0 / inner)
    du = q * m_ref[...] - u * (q * q * q * k)
    dy = du * silu
    dy_ref[...] = dy
    gz_ref[...] = (du * y * sig * (1.0 + z * (1.0 - sig))).astype(BF16)
    n = (u * q * gain_ref[...]).astype(BF16)
    c = c_ref[...]
    put(back_refs, dot_split_left(dy * jnp.exp(pair_column(cols, 3, frames)), c, 0, 0),
        dot_split_left(dy * jnp.exp(pair_column(cols, 0, frames)), c, 0, 0))
    at = 0
    for w_ref in w_refs:
        columns = w_ref.shape[1]
        w_ref[...] = dot(n, d_ref[:, at : at + columns], 0, 0) * weight_scale
        at += columns


def near_kernel(quad, order_ref, x_ref, b_ref, c_ref, cols_ref, rows_ref, skip_ref, dy_ref, *refs):
    entry = pick(refs[:quad])
    gx_ref, gb_ref, gc_ref, scores, pairs = refs[quad:]
    frames = x_ref.shape[0]
    step = pl.program_id(0)

    @pl.when(step == 0)
    def _():
        scores[...] = dot(b_ref[...], c_ref[...], 1, 1)
        pairs[...] = jnp.zeros_like(pairs)
        gc_ref[...] = jnp.zeros_like(gc_ref)

    cols, rows = cols_ref[0], rows_ref[0]
    x = x_ref[...]
    dy = dy_ref[...]
    lane = lax.broadcasted_iota(jnp.int32, (frames, PAIR), 1)
    parts = []
    for e in range(2):
        weight = pair_weights(cols, rows, e, frames, False)
        own = (lane < HEAD_DIM) if e == 0 else (lane >= HEAD_DIM)
        dy_own = jnp.where(own, dy, 0.0)
        pairs[...] += weight * dot_split_right(x, dy_own, 1, 1)
        parts.append(dot_split_both(weight * scores[...], dy_own, 1, 0))
    gx_ref[...] = parts[0] + parts[1] + skip_ref[...] * dy
    gc_ref[...] += dot_split_both(dy * jnp.exp(pair_column(cols, 0, frames)), entry[0], 1, 0)
    gc_ref[...] += dot_split_both(dy * jnp.exp(pair_column(cols, 3, frames)), entry[1], 1, 0)

    @pl.when(step == pl.num_programs(0) - 1)
    def _():
        gb_ref[...] = dot_split_left(pairs[...], c_ref[...], 1, 0)
        gc_ref[...] += dot_split_left(pairs[...], b_ref[...], 0, 0)


def far_kernel(quad, order_ref, x_ref, b_ref, cols_ref, near_ref, gb_near_ref, *refs):
    leave = pick(refs[:quad])
    gx_ref, gb_ref = refs[quad:]
    frames = x_ref.shape[0]

    @pl.when(pl.program_id(0) == 0)
    def _():
        gb_ref[...] = gb_near_ref[...]

    cols = cols_ref[0]
    b = b_ref[...]
    x = x_ref[...].astype(F32)
    tail = jnp.exp(pair_column(cols, 2, frames))
    lead = jnp.exp(pair_column(cols, 1, frames))
    far = tail * dot_split_right(b, leave[1], 1, 1) + lead * dot_split_right(b, leave[0], 1, 1)
    gx_ref[...] = (near_ref[...] + far).astype(BF16)
    gb_ref[...] += dot_split_both(x * tail, leave[1], 1, 0)
    gb_ref[...] += dot_split_both(x * lead, leave[0], 1, 0)


def call(kernel, name, order, ins, in_specs, outs, out_specs, scratch=(), flops=0):
    moved = sum(a.size * a.dtype.itemsize for a in ins) + sum(
        o.size * o.dtype.itemsize for o in outs)
    return pl.pallas_call(
        kernel,
        name=name,
        grid_spec=pltpu.PrefetchScalarGridSpec(
            num_scalar_prefetch=1,
            grid=(order.shape[0],),
            in_specs=in_specs,
            out_specs=out_specs,
            scratch_shapes=list(scratch),
        ),
        out_shape=outs,
        compiler_params=pltpu.CompilerParams(
            dimension_semantics=("arbitrary",), vmem_limit_bytes=VMEM_BYTES),
        cost_estimate=pl.CostEstimate(flops=flops, bytes_accessed=moved, transcendentals=0),
    )(order, *ins)


def small_call(kernel, name, factors, ins, outs):
    moved = sum(a.size * 4 for a in ins) + sum(o.size * 4 for o in outs)
    vmem = pl.BlockSpec(memory_space=pltpu.VMEM)
    return pl.pallas_call(
        kernel,
        name=name,
        in_specs=[pl.BlockSpec(memory_space=pltpu.SMEM)] + [vmem] * len(ins),
        out_specs=[vmem] * len(outs),
        out_shape=outs,
        compiler_params=pltpu.CompilerParams(vmem_limit_bytes=VMEM_BYTES),
        cost_estimate=pl.CostEstimate(flops=0, bytes_accessed=moved, transcendentals=0),
    )(factors, *ins)


def sum_over(value, axis):
    size = lax.axis_size(axis)
    reach = 1
    while reach < size:
        value = value + lax.ppermute(value, axis, [(i, i ^ reach) for i in range(size)])
        reach *= 2
    return value


def exchange(value, bit):
    size = lax.axis_size("seq")
    return lax.ppermute(value, "seq", [(i, i ^ (1 << bit)) for i in range(size)])


def sum_slabs(values, orders, beside):
    me = lax.axis_index("seq")
    count = len(orders[0])
    values = list(values)
    for n in range(count):
        kept, came = [], []
        for value, bits in zip(values, orders):
            mine = (me >> bits[n]) & 1
            halves = value.reshape(2, value.shape[0] // 2, value.shape[1])
            kept.append(lax.dynamic_index_in_dim(halves, mine, 0, keepdims=False))
            came.append(exchange(
                lax.dynamic_index_in_dim(halves, 1 - mine, 0, keepdims=False), bits[n]))
        came = beside(n, came)
        values = [a + b for a, b in zip(kept, came)]
        if n == 1:
            values = [jnp.concatenate(values[:2], axis=1), values[2]]
            all_orders, orders = orders, orders[1:]
    for n in reversed(range(count)):
        if n == 1:
            values = [*jnp.split(values[0], 2, axis=1), values[1]]
            orders = all_orders
        came = [exchange(value, bits[n]) for value, bits in zip(values, orders)]
        came = beside(2 * count - 1 - n, came)
        for i, (other, bits) in enumerate(zip(came, orders)):
            first = ((me >> bits[n]) & 1) == 0
            values[i] = jnp.concatenate(
                [jnp.where(first, values[i], other), jnp.where(first, other, values[i])], axis=0)
    return jnp.concatenate(values, axis=1)


def factor_reader(factors_ref, quad, heads, steps):
    kinds = 1 + 2 * quad + quad * quad + steps

    def read(d, kind, h):
        return factors_ref[(d * kinds + kind) * heads + h]

    return read


def total_kernel(quad, heads, steps, factors_ref, *refs):
    read = factor_reader(factors_ref, quad, heads, steps)
    for d in range(2):
        for h in range(heads):
            at = slice(h * HEAD_DIM, (h + 1) * HEAD_DIM)
            total = read(d, 0, h) * refs[0][d, at, :]
            for r in range(1, quad):
                total = total + read(d, r, h) * refs[r][d, at, :]
            refs[quad + d][at, :] = total


def advance_kernel(quad, heads, steps, k, factors_ref, *refs):
    read = factor_reader(factors_ref, quad, heads, steps)
    totals, came, before, sent, after = refs[:2], refs[2:4], refs[4:-4], refs[-4:-2], refs[-2:]
    for d in range(2):
        for h in range(heads):
            at = slice(h * HEAD_DIM, (h + 1) * HEAD_DIM)
            entering = came[d][at, :]
            if k:
                passed = read(d, 1 + 2 * quad + quad * quad + k, h)
                entering = before[d][at, :] + passed * entering
            after[d][at, :] = entering
            sent[d][at, :] = totals[d][at, :] + read(d, quad, h) * entering


def reply_kernel(quad, heads, steps, factors_ref, *refs):
    read = factor_reader(factors_ref, quad, heads, steps)
    held, came, before, replies = refs[:quad], refs[quad : quad + 2], refs[quad + 2 : -quad], refs[-quad:]
    k = steps - 1
    for d in range(2):
        for h in range(heads):
            at = slice(h * HEAD_DIM, (h + 1) * HEAD_DIM)
            entering = came[d][at, :]
            if k:
                passed = read(d, 1 + 2 * quad + quad * quad + k, h)
                entering = before[d][at, :] + passed * entering
            states = [held[s][d, at, :] for s in range(quad)]
            for r in range(quad):
                reply = read(d, quad + 1 + r, h) * entering
                for s in range(quad):
                    if s != r:
                        reply = reply + read(d, 1 + 2 * quad + s * quad + r, h) * states[s]
                replies[r][d, at, :] = reply


def scan_factors(ends_f, ends_b, quad, steps):
    size, me = lax.axis_size("seq"), lax.axis_index("seq")
    heads = ends_f.shape[0]
    table = jnp.concatenate([ends_f, ends_b])[None, :]
    reach = 1
    while reach < size:
        came = lax.ppermute(table, "seq", [(i, i ^ reach) for i in range(size)])
        table = jnp.concatenate([table, came], axis=0)
        reach *= 2
    none = -1
    runs = [(r, 0, none, quad) for r in range(quad)]
    runs += [(none, -1, none, quad)]
    runs += [(none, -1, r, 0) for r in range(quad)]
    runs += [(s, 0, r, 0) for s in range(quad) for r in range(quad)]
    runs += [(none, -(2 ** k - 1) * quad - 1, none, 0) for k in range(steps)]
    low_xor, low_add, high_xor, high_add = (jnp.array(v, jnp.int32) for v in zip(*runs))
    place = jnp.stack([me, size - 1 - me])[:, None]
    base = place // quad * quad
    low = jnp.where(low_xor == none, base + low_add, place ^ low_xor)
    high = jnp.where(high_xor == none, base + high_add, place ^ high_xor)
    slab = (place ^ jnp.arange(size, dtype=jnp.int32))[:, None, :]
    inside = (slab > low[:, :, None]) & (slab < high[:, :, None])
    logs = table.reshape(1, 1, size, 2 * heads)
    powers = jnp.sum(jnp.where(inside[..., None], logs, 0.0), axis=2)
    factors = jnp.where((low < high)[..., None], jnp.exp(powers), 0.0)
    return factors.reshape(2, len(runs), 2, heads)


def carry(mine, factors, quad, steps):
    size = lax.axis_size("seq")
    _, rows, width = mine[0].shape
    heads = rows // HEAD_DIM
    both = jax.ShapeDtypeStruct((2, rows, width), F32)
    one = jax.ShapeDtypeStruct((rows, width), F32)
    sizes = (quad, heads, steps)

    def trade(parts):
        return [parts[0]] + [
            lax.ppermute(parts[r], "seq", [(i, i ^ r) for i in range(size)])
            for r in range(1, quad)]

    held = yield trade(mine)
    totals = small_call(
        functools.partial(total_kernel, *sizes), "group_totals", factors, held, [one, one])
    sent, before = totals, []
    for k in range(steps):
        came = []
        for d, sign in enumerate((1, -1)):
            shift = sign * quad * 2 ** k
            came.append(lax.ppermute(
                sent[d], "seq", [(i, i + shift) for i in range(size) if 0 <= i + shift < size]))
        came = yield came
        if k < steps - 1:
            new = small_call(
                functools.partial(advance_kernel, *sizes, k), "advance_scan", factors,
                [*totals, *came, *before], [one] * 4)
            sent, before = new[:2], new[2:]
    replies = small_call(
        functools.partial(reply_kernel, *sizes), "group_replies", factors,
        [*held, *came, *before], [both] * quad)
    return (yield trade(replies))


def body(x_in, gate_in, b_in, c_in, decay_fwd, decay_bwd, skip_gain, norm_gain, w_out, d_out):
    frames, width = x_in.shape
    heads = decay_fwd.shape[0]
    state = b_in.shape[1]
    model = d_out.shape[1]
    pairs = heads // 2
    inner = width * lax.axis_size("head")

    fwd = jnp.cumsum(decay_fwd, axis=1)
    bwd = jnp.cumsum(decay_bwd, axis=1) - decay_bwd
    fwd_end = fwd[:, -1:]
    bwd_end = bwd[:, -1:] + decay_bwd[:, -1:]
    lines = jnp.stack([fwd, bwd, fwd_end - fwd, bwd_end - bwd], axis=1)
    rows = lines.reshape(pairs, 8, frames)
    cols = rows.transpose(0, 2, 1)
    quad = min(QUAD, pairs)
    per_part = pairs // quad
    part_heads = heads // quad
    slabs = lax.axis_size("seq")
    steps = (slabs // quad - 1).bit_length()
    q = lax.axis_index("seq") % quad
    turn = jnp.arange(pairs, dtype=jnp.int32)
    order = ((turn // per_part) ^ q) * per_part + turn % per_part
    factors = scan_factors(fwd_end[:, 0], bwd_end[:, 0], quad, steps)
    factors = lax.dynamic_slice_in_dim(factors, q * part_heads, part_heads, 3)
    entry_factors = jnp.stack([factors[0, :, 0], factors[1, :, 1]]).reshape(-1)
    exit_factors = jnp.stack([factors[0, :, 1], factors[1, :, 0]]).reshape(-1)
    skip = jnp.repeat(skip_gain, HEAD_DIM)[None, :]
    gain = norm_gain[None, :]

    wide = pl.BlockSpec((frames, PAIR), lambda i, p: (0, p[i]))
    narrow = pl.BlockSpec((frames, state), lambda i, p: (0, 0))
    col = pl.BlockSpec((1, frames, 8), lambda i, p: (p[i], 0, 0))
    row = pl.BlockSpec((1, 8, frames), lambda i, p: (p[i], 0, 0))
    lanes = pl.BlockSpec((1, PAIR), lambda i, p: (0, p[i]))
    states = [
        pl.BlockSpec((2, PAIR, state),
                     lambda i, p, r=r: (0, jnp.clip(i - r * per_part, 0, per_part - 1), 0))
        for r in range(quad)]
    model_rows = pl.BlockSpec((frames, model), lambda i, p: (0, 0))
    weight_rows = pl.BlockSpec((PAIR, model), lambda i, p: (p[i], 0))
    sums_spec = pl.BlockSpec((frames, 2), lambda i, p: (0, 0))
    shape = jax.ShapeDtypeStruct
    wide_f32, wide_bf16 = shape((frames, width), F32), shape((frames, width), BF16)
    state_out = [shape((2, width // quad, state), F32)] * quad
    narrow_out = shape((frames, state), F32)
    square = pltpu.VMEM((frames, frames), F32)
    lane_sums = pltpu.VMEM((frames, PAIR), F32)
    quad_flops = 2 * frames * frames * width

    local = call(state_kernel, "local_states", order, (x_in, b_in, cols), [wide, narrow, col],
                 state_out, states, flops=8 * frames * width * state)
    near_y, scaled = call(
        within_kernel, "within_slab", order,
        (x_in, b_in, c_in, cols, rows, w_out, d_out, gain, skip),
        [wide, narrow, narrow, col, row, weight_rows, model_rows, lanes, lanes],
        [wide_f32, wide_f32], [wide, wide], [square],
        flops=8 * quad_flops + 2 * frames * width * model)
    stages = carry(local, entry_factors, quad, steps)
    flying, at = next(stages), 0
    while at <= steps:
        if at == 1:
            flying, near_y, scaled = lax.optimization_barrier((flying, near_y, scaled))
        flying, at = stages.send(flying), at + 1
    entry = flying
    y, sums = call(
        functools.partial(merge_kernel, quad), "merge_entry", order,
        (near_y, scaled, gate_in, c_in, cols, *entry),
        [wide, wide, wide, narrow, col, *states],
        [wide_f32, shape((frames, 2), F32)], [wide, sums_spec], [lane_sums, lane_sums],
        flops=8 * frames * width * state)
    sums = sum_over(sums, "head")
    bits = list(range((lax.axis_size("seq") - 1).bit_length()))
    orders = (bits, [bits[1], bits[0]] + bits[2:], bits[2:] + bits[:2])
    thirds = model // 8 * 3
    chunks = (thirds, thirds, model - 2 * thirds)
    dy, grad_z, *rest = call(
        functools.partial(turn_kernel, inner, quad), "norm_backward", order,
        (y, scaled, gate_in, c_in, cols, sums, gain, d_out),
        [wide, wide, wide, narrow, col, sums_spec, lanes, model_rows],
        [wide_f32, wide_bf16, *state_out] + [shape((width, n), F32) for n in chunks],
        [wide, wide, *states] + [pl.BlockSpec((PAIR, n), lambda i, p: (p[i], 0)) for n in chunks],
        flops=2 * frames * width * model + 8 * frames * width * state)
    back, local_w = rest[:quad], rest[quad:]
    stages = carry(back, exit_factors, quad, steps)
    near_x, near_b, grad_c = call(
        functools.partial(near_kernel, quad), "near_gradients", order,
        (x_in, b_in, c_in, cols, rows, skip, dy, *entry),
        [wide, narrow, narrow, col, row, lanes, wide, *states],
        [wide_f32, narrow_out, narrow_out], [wide, narrow, narrow], [square, square],
        flops=20 * quad_flops)
    held = {"near": (near_x, near_b, grad_c)}
    last = steps + 1

    def beside(n, came):
        stage = n - 2
        if n == 0:
            came, held["near"] = lax.optimization_barrier((came, held["near"]))
        elif n == 1:
            held["c"] = sum_over(held["near"][2], "head")
            came, held["c"] = lax.optimization_barrier((came, held["c"]))
        elif stage <= last:
            flying = held["next"] if stage else next(stages)
            came, flying = lax.optimization_barrier((came, flying))
            held["next"] = flying if stage == last else stages.send(flying)
        elif stage == last + 1:
            far = call(
                functools.partial(far_kernel, quad), "far_gradients", order,
                (x_in, b_in, cols, held["near"][0], held["near"][1], *held["next"]),
                [wide, narrow, col, wide, narrow, *states],
                [wide_bf16, narrow_out], [wide, narrow], flops=20 * frames * width * state)
            came, held["far"] = lax.optimization_barrier((came, far))
        elif stage == last + 2:
            held["b"] = sum_over(held["far"][1], "head")
            came, held["b"] = lax.optimization_barrier((came, held["b"]))
        return came

    grad_w = sum_slabs(local_w, orders, beside)
    return held["far"][0], grad_z, held["b"], held["c"], grad_w


def solution(mesh):
    in_specs = (
        P("seq", "head"),
        P("seq", "head"),
        P("seq", None),
        P("seq", None),
        P("head", "seq"),
        P("head", "seq"),
        P("head"),
        P("head"),
        P("head", None),
        P("seq", None),
    )
    out_specs = (
        P("seq", "head"),
        P("seq", "head"),
        P("seq", None),
        P("seq", None),
        P("head", None),
    )
    return jax.shard_map(body, mesh=mesh, in_specs=in_specs, out_specs=out_specs, check_vma=False)
```
